32 devices in a mesh: rep: 2 (over y), fsdp: 16 (over z, x, core).
Axes of the slice: x: 2, y: 2, z: 4, core: 2. Of those that a mesh axis runs over, the one named last changes fastest.
Arguments:
- x_in: bfloat16 [2, 2048, 512], P('rep', 'fsdp'), may hold values from -8 to 8
- d_out: bfloat16 [2, 2048, 512], P('rep', 'fsdp'), may hold values from -0.375 to 0.375
- gate_weight: bfloat16 [64, 128, 128], P('fsdp'), may hold values from -0.25 to 0.25
- up_weight: bfloat16 [64, 128, 128], P('fsdp'), may hold values from -0.25 to 0.25
- down_weight: bfloat16 [64, 128, 128], P('fsdp'), may hold values from -0.125 to 0.125
- mom_gate: float32 [2, 64, 128, 128], P('rep', 'fsdp'), may hold values from -6 to 6
- mom_up: float32 [2, 64, 128, 128], P('rep', 'fsdp'), may hold values from -6 to 6
- mom_down: float32 [2, 64, 128, 128], P('rep', 'fsdp'), may hold values from -6 to 6
- band_index: int32 [3, 64, 512], P(None, 'fsdp'), may hold values from 0 to 16383, as said below
Outputs:
- res_gate: float32 [2, 64, 128, 128], P('rep', 'fsdp')
- res_up: float32 [2, 64, 128, 128], P('rep', 'fsdp')
- down_residual_blocks: float32 [2, 64, 128, 128], P('rep', 'fsdp')
- upd_gate: float32 [64, 128, 128], P('fsdp')
- upd_up: float32 [64, 128, 128], P('fsdp')
- upd_down: float32 [64, 128, 128], P('fsdp')
The draws below stay inside these ranges and needn't reach their ends.
Inputs may be any that keep to these rules, and one draw needn't show every extreme that they name: `band_index`: each row of 512 positions of a block holds distinct values; the positions are the same for every replica group.
All inputs are finite; a program needn't handle non-finite values.
Results may differ from the reference program's by a relative error of at most 0.0028.
Values may be sent and summed in bfloat16 or wider, within the bound.
No kernel may reach another device: no remote copies, remote signals or barrier semaphores. Data moves between devices by JAX's collectives and lax.ppermute only.
A program may use at most 128 MiB of HBM per device.

```python
import jax
import jax.numpy as jnp
from jax import lax

D = 512
FF = 2048
SPAN = 128
K = 512
TOKENS = 2048
MATRIX_PARTS = 64
N_REP = 2


def draw_band_index(key, part):
    key = jax.random.fold_in(key, 11)
    row_keys = jax.random.split(key, 3 * MATRIX_PARTS)

    def one_row(row_key):
        return jax.random.permutation(row_key, SPAN * SPAN)[:K]
    chosen = jax.vmap(one_row)(row_keys)
    return chosen.reshape(3, MATRIX_PARTS, K).astype(jnp.int32)


def strengthened(drawn, stream_key, source, target, blocks, factor):
    owner, partner = [(jnp.arange(drawn.shape[position]) // (drawn.shape[position] // blocks)).reshape([-1 if axis == position else 1 for axis in range(drawn.ndim)]) for position in (source, target)]
    chosen = jax.random.permutation(stream_key, blocks)[partner]
    strong = (owner == chosen) | (owner == (partner + blocks // 2) % blocks)
    return jnp.where(strong, factor * drawn, drawn)


def levels(own_key, extent, pieces, low, largest):
    def one(dim, shards_of):
        heights = jax.random.uniform(jax.random.fold_in(jax.random.fold_in(own_key, 6), dim), (shards_of,), jnp.float32, low / len(pieces), largest / len(pieces))
        return jnp.repeat(jnp.exp(heights), extent[dim] // shards_of).reshape((-1,) + (1,) * (len(extent) - dim - 1))

    gain = one(*pieces[0])
    for cut in pieces[1:]:
        gain = gain * one(*cut)
    return gain


def scatter_about(key, extent, width, most, cuts=(), held_as=jnp.bfloat16):
    values = width * jax.random.normal(key, extent, jnp.float32)
    if cuts:
        values = values * levels(key, extent, cuts, -0.22, 0.18)
    return jnp.clip(values, -most, most).astype(held_as)


def noise_with(own_key, dims, deviation, bound, cuts, heavy, kind=jnp.bfloat16):
    drawn = deviation * jax.random.normal(own_key, dims, jnp.float32)
    if cuts:
        drawn = drawn * levels(own_key, dims, cuts, -0.22, 0.18)
    return jnp.clip(strengthened(drawn, jax.random.fold_in(own_key, 3), *heavy), -bound, bound).astype(kind)


def setup_inputs(seed: int = 0) -> dict:
    streams_of = jax.random.split(jax.random.key(seed), 10)
    x_in = noise_with(streams_of[0], (N_REP, TOKENS, D), 1.0, 8.0, ((0, 2), (1, 16)), (1, 2, 16, 2.0))
    d_out = noise_with(streams_of[1], (N_REP, TOKENS, D), ((FF / (D * TOKENS)) ** 0.5), 0.375, ((0, 2), (1, 16)), (1, 2, 16, 2.0))
    gate_weight = scatter_about(streams_of[2], (MATRIX_PARTS, SPAN, SPAN), D ** -0.5, 0.25, ((0, 16),))
    up_weight = scatter_about(streams_of[3], (MATRIX_PARTS, SPAN, SPAN), D ** -0.5, 0.25, ((0, 16),))
    down_weight = scatter_about(streams_of[4], (MATRIX_PARTS, SPAN, SPAN), FF ** -0.5, 0.125, ((0, 16),))
    mom_gate = scatter_about(streams_of[5], (N_REP, MATRIX_PARTS, SPAN, SPAN), 1.0, 6.0, ((0, 2), (1, 16)), jnp.float32)
    mom_up = scatter_about(streams_of[6], (N_REP, MATRIX_PARTS, SPAN, SPAN), 1.0, 6.0, ((0, 2), (1, 16)), jnp.float32)
    mom_down = scatter_about(streams_of[7], (N_REP, MATRIX_PARTS, SPAN, SPAN), 1.0, 6.0, ((0, 2), (1, 16)), jnp.float32)
    band_index = draw_band_index(jax.random.fold_in(streams_of[9], 71), 0)
    return {"x_in": x_in, "d_out": d_out, "gate_weight": gate_weight, "up_weight": up_weight, "down_weight": down_weight, "mom_gate": mom_gate, "mom_up": mom_up, "mom_down": mom_down, "band_index": band_index}


momentum_decay = 0.999

def dct_table(side_len):
    freq_rows = jnp.arange(side_len, dtype=jnp.float32)[:, None]
    cell_cols = jnp.arange(side_len, dtype=jnp.float32)[None, :]
    weights = jnp.where(freq_rows == 0, jnp.sqrt(1.0 / side_len), jnp.sqrt(2.0 / side_len))
    return weights * jnp.cos(jnp.pi * (2.0 * cell_cols + 1.0) * freq_rows / (2.0 * side_len))

def forward_blocks(cosines, blocks):
    inner = jnp.matmul(cosines, blocks, precision=lax.Precision.HIGHEST)
    return jnp.matmul(inner, cosines.T, precision=lax.Precision.HIGHEST)

def inverse_blocks(cosines, coeffs):
    inner = jnp.matmul(cosines.T, coeffs, precision=lax.Precision.HIGHEST)
    return jnp.matmul(inner, cosines, precision=lax.Precision.HIGHEST)

def place_band(values, positions, side_len):
    layout = (positions.shape[0], positions.shape[1], side_len * side_len)
    matrix_ids = jnp.arange(layout[0])[:, None, None]
    span_ids = jnp.arange(layout[1])[None, :, None]
    filled = jnp.zeros(layout, values.dtype).at[matrix_ids, span_ids, positions].set(values)
    return filled.reshape(layout[0], layout[1], side_len, side_len)

def band_split(moments, gradients, band_index):
    side_len = moments.shape[2]
    updated = momentum_decay * moments + gradients
    cosines = dct_table(side_len)
    coeffs = forward_blocks(cosines, updated)
    flattened = coeffs.reshape(coeffs.shape[0], coeffs.shape[1], side_len * side_len)
    picked = jnp.take_along_axis(flattened, band_index, axis=2)
    kept_part = inverse_blocks(cosines, place_band(picked, band_index, side_len))
    return (updated - kept_part, picked)

def decode_band(summed, band_index, side_len):
    cosines = dct_table(side_len)
    return inverse_blocks(cosines, place_band(summed, band_index, side_len))

def input_full(blocks, row_blocks, col_blocks):
    side_len = blocks.shape[1]
    grid = blocks.reshape(col_blocks, row_blocks, side_len, side_len)
    return grid.transpose(1, 2, 0, 3).reshape(row_blocks * side_len, col_blocks * side_len)

def output_full(blocks, row_blocks, col_blocks):
    side_len = blocks.shape[1]
    grid = blocks.reshape(col_blocks, row_blocks, side_len, side_len)
    return grid.transpose(0, 2, 1, 3).reshape(col_blocks * side_len, row_blocks * side_len)

def input_blocks(matrix, side_len):
    row_blocks = matrix.shape[0] // side_len
    col_blocks = matrix.shape[1] // side_len
    grid = matrix.reshape(row_blocks, side_len, col_blocks, side_len).transpose(2, 0, 1, 3)
    return grid.reshape(row_blocks * col_blocks, side_len, side_len)

def output_blocks(matrix, side_len):
    col_blocks = matrix.shape[0] // side_len
    row_blocks = matrix.shape[1] // side_len
    grid = matrix.reshape(col_blocks, side_len, row_blocks, side_len).transpose(0, 2, 1, 3)
    return grid.reshape(row_blocks * col_blocks, side_len, side_len)

def reference(x_in, d_out, gate_weight, up_weight, down_weight, mom_gate, mom_up, mom_down, band_index):
    side_len = gate_weight.shape[1]
    row_blocks = x_in.shape[2] // side_len
    col_blocks = gate_weight.shape[0] // row_blocks
    gate_whole = input_full(gate_weight, row_blocks, col_blocks)
    up_whole = input_full(up_weight, row_blocks, col_blocks)
    down_whole = output_full(down_weight, row_blocks, col_blocks)

    def per_group(group_items):
        x_rows, d_rows, moment_gate, up_momentum, moment_down = group_items
        gate_pre = jnp.dot(x_rows, gate_whole, preferred_element_type=jnp.float32)
        up_pre = jnp.dot(x_rows, up_whole, preferred_element_type=jnp.float32)
        d_hidden = jnp.dot(d_rows, down_whole.T, preferred_element_type=jnp.float32)
        sigmoid_gate = jax.nn.sigmoid(gate_pre)
        hidden = (gate_pre * sigmoid_gate * up_pre).astype(jnp.bfloat16)
        d_gate = (d_hidden * up_pre * sigmoid_gate * (1.0 + gate_pre * (1.0 - sigmoid_gate))).astype(jnp.bfloat16)
        d_up = (d_hidden * gate_pre * sigmoid_gate).astype(jnp.bfloat16)
        grad_gate = jnp.dot(x_rows.T, d_gate, preferred_element_type=jnp.float32)
        grad_up = jnp.dot(x_rows.T, d_up, preferred_element_type=jnp.float32)
        grad_down = jnp.dot(hidden.T, d_rows, preferred_element_type=jnp.float32)
        gradients = jnp.stack([input_blocks(grad_gate, side_len), input_blocks(grad_up, side_len), output_blocks(grad_down, side_len)])
        moments = jnp.stack([moment_gate, up_momentum, moment_down])
        return band_split(moments, gradients, band_index)
    remains, picked = lax.map(per_group, (x_in, d_out, mom_gate, mom_up, mom_down))
    summed = lax.optimization_barrier(jnp.sum(picked, axis=0))
    updates = decode_band(summed, band_index, side_len)
    return (remains[:, 0], remains[:, 1], remains[:, 2], updates[0], updates[1], updates[2])
```

```python
import functools

import jax
import jax.numpy as jnp
import numpy as np
from jax import lax
from jax.experimental import pallas as pl
from jax.experimental.pallas import tpu as pltpu
from jax.sharding import PartitionSpec as P

MOMENTUM_DECAY = 0.999
LATE_FLOPS = 4 * 10**9
TABLES_FLOPS = 10**9
F32 = jnp.float32
BF16 = jnp.bfloat16


def dct_table(side):
    k = np.arange(side, dtype=np.float64)[:, None]
    n = np.arange(side, dtype=np.float64)[None, :]
    scale = np.where(k == 0, np.sqrt(1.0 / side), np.sqrt(2.0 / side))
    return (scale * np.cos(np.pi * (2.0 * n + 1.0) * k / (2.0 * side))).astype(np.float32)


def split2(value):
    hi = value.astype(BF16)
    return hi, (value - hi.astype(F32)).astype(BF16)


def dot(a, b):
    return jnp.dot(a, b, preferred_element_type=F32)


def dot_nt(a, b):
    return lax.dot_general(a, b, (((1,), (1,)), ((), ())), preferred_element_type=F32)


def dot3(a, b):
    a_hi, a_lo = split2(a)
    b_hi, b_lo = split2(b)
    left = jnp.concatenate([a_hi, a_hi, a_lo], axis=1)
    return dot(left, jnp.concatenate([b_hi, b_lo, b_hi], axis=0))


def lanes_to_rows(value, side):
    count = value.shape[1] // side
    return jnp.concatenate([value[:, i * side : (i + 1) * side] for i in range(count)], axis=0)


def decode(values, in_row_ref, cells_ref, cosines_t):
    side = cosines_t.shape[0]
    inner = []
    for b, row in enumerate(values):
        hi, lo = split2(row)
        in_row = in_row_ref[b]
        both = dot(jnp.concatenate([in_row * hi, in_row * lo], axis=0), cells_ref[b])
        inner.append(both[:side, :side] + (both[:side, side:] + both[side:, :side]))
    return dot3(cosines_t, jnp.concatenate(inner, axis=1))


def activations(wgu, wd, x, d):
    pre = dot_nt(wgu, x)
    dh = dot_nt(wd, d)
    gate, up = pre[: wd.shape[0]], pre[wd.shape[0] :]
    sig = 1.0 / (1.0 + jnp.exp(-gate))
    swish = gate * sig
    d_gate = (dh * up * sig * (1.0 + gate * (1.0 - sig))).astype(BF16)
    return d_gate, (dh * swish).astype(BF16), (swish * up).astype(BF16)


def tables_kernel(index_ref, cosines_ref, in_row_ref, in_col_ref, cells_ref):
    side = cosines_ref.shape[0]
    parts = jnp.concatenate(split2(cosines_ref[...]), axis=1)
    shift = int(np.log2(side))
    matrices, count, keep = index_ref.shape
    lines = lax.broadcasted_iota(jnp.int32, (side, keep), 0)
    for m in range(matrices):
        for i in range(count):
            b = m * count + i
            index = index_ref[m, i : i + 1, :]
            in_col = jnp.where((index & (side - 1)) == lines, 1.0, 0.0).astype(BF16)
            in_row_ref[b] = jnp.where((index >> shift) == lines, 1.0, 0.0).astype(BF16)
            in_col_ref[b] = in_col
            cells_ref[b] = dot(in_col.T, parts).astype(BF16)


def early_kernel(shards, *refs):
    xs, ds, weights = refs[:shards], refs[shards : 2 * shards], refs[2 * shards : 2 * shards + 2]
    own_ref, par_ref, wgu_ref, wd_ref, x_all, d_all, act = refs[2 * shards + 2 :]
    rows = xs[0].shape[0]
    side = own_ref.shape[1]
    count = weights[0].shape[0] // 3
    for i in range(count):
        cols = slice(i * side, (i + 1) * side)
        for p in range(2):
            gate, up, down = (weights[p][m * count + i] for m in range(3))
            wgu_ref[p * side : (p + 1) * side, cols] = gate.T
            wgu_ref[(2 + p) * side : (3 + p) * side, cols] = up.T
            wd_ref[p * side : (p + 1) * side, cols] = down
    wgu, wd = wgu_ref[...], wd_ref[...]
    for s in range(0, shards, 2):
        some = range(s, min(s + 2, shards))
        x = jnp.concatenate([xs[j][...] for j in some], axis=0)
        d = jnp.concatenate([ds[j][...] for j in some], axis=0)
        span = pl.ds(s * rows, len(some) * rows)
        x_all[span, :] = x
        d_all[span, :] = d
        d_gate, d_up, hidden = activations(wgu, wd, x, d)
        act[: 2 * side, span] = d_gate
        act[2 * side : 4 * side, span] = d_up
        act[4 * side :, span] = hidden
    g_in = dot(act[: 4 * side, :], x_all[...])
    g_out = dot(act[4 * side :, :], d_all[...])
    for m, grad in enumerate((g_in[: 2 * side], g_in[2 * side :], g_out)):
        own_ref[m] = grad[:side]
        par_ref[m] = grad[side:]


def moment_step(
    grads, mom_refs, in_row_ref, in_col_ref, cosines_ref, cosines_t_ref, moment_ref, band_ref
):
    side = cosines_ref.shape[0]
    count = mom_refs[0].shape[0]
    blocks = []
    for m in range(3):
        for i in range(count):
            piece = grads[m][:, i * side : (i + 1) * side]
            if m < 2:
                piece = piece.T
            block = MOMENTUM_DECAY * mom_refs[m][i] + piece
            moment_ref[m * count + i] = block
            blocks.append(block)
    inner = dot3(cosines_ref[...], jnp.concatenate(blocks, axis=1))
    coeffs = dot3(lanes_to_rows(inner, side), cosines_t_ref[...])
    for m in range(3):
        for i in range(count):
            b = m * count + i
            hi, lo = split2(coeffs[b * side : (b + 1) * side])
            in_col = in_col_ref[b]
            at_col = dot(jnp.concatenate([hi, lo], axis=1), jnp.concatenate([in_col, in_col], axis=0))
            band_ref[m, i : i + 1, :] = jnp.sum(
                at_col * in_row_ref[b].astype(F32), axis=0, keepdims=True
            )


def late_kernel(x_ref, d_ref, wgu_ref, wd_ref, own_ref, par_ref):
    side = own_ref.shape[1]
    x, d = x_ref[...], d_ref[...]
    d_gate, d_up, hidden = activations(wgu_ref[...], wd_ref[...], x, d)
    for m, grad in enumerate((dot(d_gate, x), dot(d_up, x), dot(hidden, d))):
        own_ref[m] = grad[:side]
        par_ref[m] = grad[side:].astype(BF16)


def moment_kernel(terms, *refs):
    grads = [sum(ref[m].astype(F32) for ref in refs[:terms]) for m in range(3)]
    moment_step(grads, refs[terms : terms + 3], *refs[terms + 3 :])


def residual_kernel(moment_ref, band_ref, in_row_ref, cells_ref, cosines_t_ref, *outs):
    side = cosines_t_ref.shape[0]
    count = outs[0].shape[0]
    pairs = [(m, i) for m in range(3) for i in range(count)]
    values = [band_ref[m, i : i + 1, :] for m, i in pairs]
    decoded = decode(values, in_row_ref, cells_ref, cosines_t_ref[...])
    for b, (m, i) in enumerate(pairs):
        kept = decoded[:, b * side : (b + 1) * side]
        outs[3][b] = kept
        outs[m][i] = moment_ref[b] - kept


def update_kernel(kept_ref, other_ref, in_row_ref, cells_ref, cosines_t_ref, *outs):
    side = cosines_t_ref.shape[0]
    count = outs[0].shape[0]
    pairs = [(m, i) for m in range(3) for i in range(count)]
    values = [
        sum(other_ref[g, m, i : i + 1, :] for g in range(other_ref.shape[0])) for m, i in pairs
    ]
    decoded = decode(values, in_row_ref, cells_ref, cosines_t_ref[...])
    for b, (m, i) in enumerate(pairs):
        outs[m][i] = kept_ref[b] + decoded[:, b * side : (b + 1) * side]


def call(kernel, out_shape, flops, *args, scratch=(), in_place={}):
    moved = sum(a.size * a.dtype.itemsize for a in args)
    specs = [
        pl.BlockSpec(memory_space=in_place.get(k, pltpu.VMEM)) for k in range(len(args))
    ]
    return pl.pallas_call(
        kernel,
        out_shape=out_shape,
        in_specs=specs,
        scratch_shapes=list(scratch),
        compiler_params=pltpu.CompilerParams(vmem_limit_bytes=24 * 1024 * 1024),
        cost_estimate=pl.CostEstimate(flops=flops, bytes_accessed=2 * moved, transcendentals=0),
    )(*args)


def ring_perms(count):
    chips = count // 2
    order = list(range(0, chips, 2)) + list(range(1, chips, 2))[::-1]
    forward = [
        (2 * order[p] + c, 2 * order[(p + 1) % chips] + c) for p in range(chips) for c in range(2)
    ]
    return forward, [(b, a) for a, b in forward], chips


def band_tables(band_index, cosines):
    blocks, keep, side = band_index.shape[0] * band_index.shape[1], band_index.shape[2], cosines.shape[0]
    return call(
        tables_kernel,
        (
            jax.ShapeDtypeStruct((blocks, side, keep), BF16),
            jax.ShapeDtypeStruct((blocks, side, keep), BF16),
            jax.ShapeDtypeStruct((blocks, keep, 2 * side), BF16),
        ),
        TABLES_FLOPS,
        band_index,
        cosines,
    )


def column_moments(x, d, weights, momenta, tables, cosines, cosines_t, shapes):
    side = weights[0].shape[1]
    rows, width = x.shape
    count = lax.axis_size("fsdp")
    swap = [(f, f ^ 1) for f in range(count)]
    forward, back, chips = ring_perms(count)

    def send(value, perm):
        return lax.ppermute(value, "fsdp", perm)

    xf, db, df, xb = send(x, forward), send(d, back), send(d, forward), send(x, back)
    xs, ds = [x, xf, xb], [d, df, db]
    own_weights = jnp.concatenate(weights, axis=0)
    partner_weights = send(own_weights, swap)
    in_row, in_col, cells = tables
    for hop in range(2, chips // 2):
        if hop == 3:
            db, in_col = lax.optimization_barrier((db, in_col))
        xf, db, df, xb = send(xf, forward), send(db, back), send(df, forward), send(xb, back)
        xs += [xf, xb]
        ds += [df, db]
    x_last, d_last = send(xf, forward), send(db, back)

    early = len(xs)
    tokens = early * rows
    part = jax.ShapeDtypeStruct((3, side, width), F32)
    own, partner, wgu, wd = call(
        functools.partial(early_kernel, early),
        (
            part,
            part,
            jax.ShapeDtypeStruct((4 * side, width), BF16),
            jax.ShapeDtypeStruct((2 * side, width), BF16),
        ),
        24 * tokens * width * side,
        *xs,
        *ds,
        own_weights,
        partner_weights,
        scratch=(
            pltpu.VMEM((tokens, width), BF16),
            pltpu.VMEM((tokens, width), BF16),
            pltpu.VMEM((6 * side, tokens), BF16),
        ),
    )
    own_late, partner_late = call(
        late_kernel,
        (part, jax.ShapeDtypeStruct(part.shape, BF16)),
        LATE_FLOPS,
        x_last,
        d_last,
        wgu,
        wd,
    )
    return call(
        functools.partial(moment_kernel, 4),
        shapes,
        10**9,
        own,
        send(partner, swap),
        own_late,
        send(partner_late, swap),
        *momenta,
        in_row,
        in_col,
        cosines,
        cosines_t,
    )


def shared_column_moments(x, d, weights, momenta, tables, cosines, cosines_t, shapes):
    gate_weight, up_weight, down_weight = weights
    own = shared_column_grads(x, d, gate_weight, up_weight, down_weight)
    return call(
        functools.partial(moment_kernel, 1), shapes, 0, own, *momenta, *tables[:2], cosines, cosines_t
    )


def shared_column_grads(x, d, gate_weight, up_weight, down_weight):
    side = gate_weight.shape[1]
    width = x.shape[1]
    blk_dev = gate_weight.shape[0]
    count = lax.axis_size("fsdp")
    share = width // side // blk_dev
    groups = [list(range(g * share, (g + 1) * share)) for g in range(count // share)]

    def whole(w):
        return lax.all_gather(w, "fsdp", axis=0, tiled=True, axis_index_groups=groups)

    gate, up = whole(gate_weight).reshape(width, side), whole(up_weight).reshape(width, side)
    down = whole(down_weight).transpose(1, 0, 2).reshape(side, width)
    x_all = lax.all_gather(x, "fsdp", axis=0, tiled=True)
    d_all = lax.all_gather(d, "fsdp", axis=0, tiled=True)
    gate_pre = jnp.dot(x_all, gate, preferred_element_type=F32)
    up_pre = jnp.dot(x_all, up, preferred_element_type=F32)
    d_hidden = jnp.dot(d_all, down.T, preferred_element_type=F32)
    sig = jax.nn.sigmoid(gate_pre)
    hidden = (gate_pre * sig * up_pre).astype(BF16)
    d_gate = (d_hidden * up_pre * sig * (1.0 + gate_pre * (1.0 - sig))).astype(BF16)
    d_up = (d_hidden * gate_pre * sig).astype(BF16)
    start = lax.rem(lax.axis_index("fsdp"), share) * blk_dev * side
    x_own = lax.dynamic_slice_in_dim(x_all, start, blk_dev * side, axis=1)
    d_own = lax.dynamic_slice_in_dim(d_all, start, blk_dev * side, axis=1)
    own = jnp.stack(
        [
            jnp.dot(d_gate.T, x_own, preferred_element_type=F32),
            jnp.dot(d_up.T, x_own, preferred_element_type=F32),
            jnp.dot(hidden.T, d_own, preferred_element_type=F32),
        ]
    )
    return own


def per_device(
    x_in, d_out, gate_weight, up_weight, down_weight, mom_gate, mom_up, mom_down, band_index
):
    side = gate_weight.shape[1]
    blk_dev = gate_weight.shape[0]
    row_blocks = x_in.shape[2] // side
    if blk_dev == row_blocks and lax.axis_size("fsdp") % 4 == 0:
        step = column_moments
    else:
        step = shared_column_moments
    cosines, cosines_t = jnp.asarray(dct_table(side)), jnp.asarray(dct_table(side).T)
    blocks = 3 * blk_dev
    dense = jax.ShapeDtypeStruct((blocks, side, side), F32)
    in_row, in_col, cells = band_tables(band_index, cosines)
    moment, band = step(
        x_in[0],
        d_out[0],
        (gate_weight, up_weight, down_weight),
        (mom_gate[0], mom_up[0], mom_down[0]),
        (in_row, in_col, cells),
        cosines,
        cosines_t,
        (dense, jax.ShapeDtypeStruct(band_index.shape, F32)),
    )
    reps = lax.axis_size("rep")
    other = jnp.stack(
        [
            lax.ppermute(band, "rep", [(r, (r + s) % reps) for r in range(reps)])
            for s in range(1, reps)
        ]
    )
    result = jax.ShapeDtypeStruct((blk_dev, side, side), F32)
    flops = 4 * 3 * blocks * side**3
    *residuals, kept = call(
        residual_kernel, (result,) * 3 + (dense,), flops, moment, band, in_row, cells, cosines_t
    )
    updates = call(
        update_kernel, (result,) * 3, flops, kept, other, in_row, cells, cosines_t
    )
    return (*(r[None] for r in residuals), *updates)


def solution(mesh):
    in_specs = (
        P("rep", "fsdp", None),
        P("rep", "fsdp", None),
        P("fsdp", None, None),
        P("fsdp", None, None),
        P("fsdp", None, None),
        P("rep", "fsdp", None, None),
        P("rep", "fsdp", None, None),
        P("rep", "fsdp", None, None),
        P(None, "fsdp", None),
    )
    out_specs = (
        P("rep", "fsdp", None, None),
        P("rep", "fsdp", None, None),
        P("rep", "fsdp", None, None),
        P("fsdp", None, None),
        P("fsdp", None, None),
        P("fsdp", None, None),
    )
    return jax.shard_map(
        per_device, mesh=mesh, in_specs=in_specs, out_specs=out_specs, check_vma=False
    )
```

```python
import functools

import jax
import jax.numpy as jnp
import numpy as np
from jax import lax
from jax.experimental import pallas as pl
from jax.experimental.pallas import tpu as pltpu
from jax.sharding import PartitionSpec as P

MOMENTUM_DECAY = 0.999
LATE_FLOPS = 4 * 10**9
TABLES_FLOPS = 10**9
PAUSE_FLOPS = 10**9
F32 = jnp.float32
BF16 = jnp.bfloat16


def dct_table(side):
    k = np.arange(side, dtype=np.float64)[:, None]
    n = np.arange(side, dtype=np.float64)[None, :]
    scale = np.where(k == 0, np.sqrt(1.0 / side), np.sqrt(2.0 / side))
    return (scale * np.cos(np.pi * (2.0 * n + 1.0) * k / (2.0 * side))).astype(np.float32)


def split2(value):
    hi = value.astype(BF16)
    return hi, (value - hi.astype(F32)).astype(BF16)


def dot(a, b):
    return jnp.dot(a, b, preferred_element_type=F32)


def dot_nt(a, b):
    return lax.dot_general(a, b, (((1,), (1,)), ((), ())), preferred_element_type=F32)


def dot3(a, b):
    a_hi, a_lo = split2(a)
    b_hi, b_lo = split2(b)
    left = jnp.concatenate([a_hi, a_hi, a_lo], axis=1)
    return dot(left, jnp.concatenate([b_hi, b_lo, b_hi], axis=0))


def lanes_to_rows(value, side):
    count = value.shape[1] // side
    return jnp.concatenate([value[:, i * side : (i + 1) * side] for i in range(count)], axis=0)


def activations(wgu, wd, x, d):
    pre = dot_nt(wgu, x)
    dh = dot_nt(wd, d)
    gate, up = pre[: wd.shape[0]], pre[wd.shape[0] :]
    sig = 1.0 / (1.0 + jnp.exp(-gate))
    swish = gate * sig
    d_gate = (dh * up * sig * (1.0 + gate * (1.0 - sig))).astype(BF16)
    return d_gate, (dh * swish).astype(BF16), (swish * up).astype(BF16)


def tables_kernel(index_ref, _, in_row_ref, in_col_ref, in_col_t_ref, mask_ref):
    side = mask_ref.shape[1]
    shift = int(np.log2(side))
    matrices, count, keep = index_ref.shape
    lines = lax.broadcasted_iota(jnp.int32, (side, keep), 0)
    for m in range(matrices):
        for i in range(count):
            b = m * count + i
            index = index_ref[m, i : i + 1, :]
            in_row = jnp.where((index >> shift) == lines, 1.0, 0.0).astype(BF16)
            in_col = jnp.where((index & (side - 1)) == lines, 1.0, 0.0).astype(BF16)
            in_col_t = in_col.T
            in_row_ref[b] = in_row
            in_col_ref[b] = in_col
            in_col_t_ref[b] = in_col_t
            mask_ref[b] = dot(in_row, in_col_t).astype(BF16)


def pause_kernel(out_ref):
    out_ref[...] = jnp.zeros_like(out_ref)


def column_grads(xs, ds, wgu, wd, x_all, d_all, act):
    rows, half = xs[0].shape[0], wd.shape[0]
    for s in range(0, len(xs), 2):
        some = range(s, min(s + 2, len(xs)))
        x = jnp.concatenate([xs[j][...] for j in some], axis=0)
        d = jnp.concatenate([ds[j][...] for j in some], axis=0)
        span = pl.ds(s * rows, len(some) * rows)
        x_all[span, :] = x
        d_all[span, :] = d
        d_gate, d_up, hidden = activations(wgu, wd, x, d)
        act[:half, span] = d_gate
        act[half : 2 * half, span] = d_up
        act[2 * half :, span] = hidden
    g_in = dot(act[: 2 * half, :], x_all[...])
    return g_in[:half], g_in[half:], dot(act[2 * half :, :], d_all[...])


def early_kernel(shards, *refs):
    xs, ds, weights = refs[:shards], refs[shards : 2 * shards], refs[2 * shards : 2 * shards + 6]
    own_ref, par_ref, wgu_ref, wd_ref, *scratch = refs[2 * shards + 7 :]
    count, side, _ = weights[0].shape
    for i in range(count):
        cols = slice(i * side, (i + 1) * side)
        for p in range(2):
            gate, up, down = (ref[i] for ref in weights[3 * p : 3 * p + 3])
            wgu_ref[p * side : (p + 1) * side, cols] = gate.T
            wgu_ref[(2 + p) * side : (3 + p) * side, cols] = up.T
            wd_ref[p * side : (p + 1) * side, cols] = down
    for m, grad in enumerate(column_grads(xs, ds, wgu_ref[...], wd_ref[...], *scratch)):
        own_ref[m] = grad[:side]
        par_ref[m] = grad[side:]


def middle_kernel(shards, *refs):
    xs, ds = refs[:shards], refs[shards : 2 * shards]
    wgu_ref, wd_ref, own_in, par_in, own_ref, par_ref, *scratch = refs[2 * shards :]
    side = own_ref.shape[1]
    for m, grad in enumerate(column_grads(xs, ds, wgu_ref[...], wd_ref[...], *scratch)):
        own_ref[m] = own_in[m] + grad[:side]
        par_ref[m] = par_in[m] + grad[side:]


def moment_step(
    grads, mom_refs, in_row_ref, in_col_ref, mask_ref, cosines_ref, cosines_t_ref, moment_ref, kept_ref, band_ref
):
    side = cosines_ref.shape[0]
    count = mom_refs[0].shape[0]
    blocks = []
    for m in range(3):
        for i in range(count):
            piece = grads[m][:, i * side : (i + 1) * side]
            if m < 2:
                piece = piece.T
            block = MOMENTUM_DECAY * mom_refs[m][i] + piece
            moment_ref[m * count + i] = block
            blocks.append(block)
    inner = dot3(cosines_ref[...], jnp.concatenate(blocks, axis=1))
    coeffs = dot3(lanes_to_rows(inner, side), cosines_t_ref[...])
    for m in range(3):
        for i in range(count):
            b = m * count + i
            block = coeffs[b * side : (b + 1) * side]
            kept_ref[b] = block * mask_ref[b].astype(F32)
            hi, lo = split2(block)
            in_col = in_col_ref[b]
            at_col = dot(jnp.concatenate([hi, lo], axis=1), jnp.concatenate([in_col, in_col], axis=0))
            band_ref[m, i : i + 1, :] = jnp.sum(
                at_col * in_row_ref[b].astype(F32), axis=0, keepdims=True
            )


def late_kernel(x_ref, d_ref, wgu_ref, wd_ref, own_ref, par_ref):
    side = own_ref.shape[1]
    x, d = x_ref[...], d_ref[...]
    d_gate, d_up, hidden = activations(wgu_ref[...], wd_ref[...], x, d)
    for m, grad in enumerate((dot(d_gate, x), dot(d_up, x), dot(hidden, d))):
        own_ref[m] = grad[:side]
        par_ref[m] = grad[side:].astype(BF16)


def moment_kernel(terms, *refs):
    grads = [sum(ref[m].astype(F32) for ref in refs[:terms]) for m in range(3)]
    moment_step(grads, refs[terms : terms + 3], *refs[terms + 3 :])


def residual_kernel(moment_ref, kept_ref, in_col_t_ref, cosines_ref, cosines_t_ref, *outs):
    *residuals, decoded_ref, cells_ref = outs
    side = cosines_ref.shape[0]
    count = residuals[0].shape[0]
    blocks = range(3 * count)
    cosines = cosines_ref[...]
    inner = dot3(jnp.concatenate([kept_ref[b] for b in blocks], axis=0), cosines)
    inner = jnp.concatenate([inner[b * side : (b + 1) * side] for b in blocks], axis=1)
    decoded = dot3(cosines_t_ref[...], inner)
    for b in blocks:
        kept = decoded[:, b * side : (b + 1) * side]
        decoded_ref[b] = kept
        residuals[b // count][b % count] = moment_ref[b] - kept
    parts = jnp.concatenate(split2(cosines), axis=1)
    for b in blocks:
        cells_ref[b] = dot(in_col_t_ref[b], parts).astype(BF16)


def update_kernel(decoded_ref, other_ref, in_row_ref, cells_ref, cosines_t_ref, *outs):
    side = cosines_t_ref.shape[0]
    count = outs[0].shape[0]
    inner = []
    for b in range(3 * count):
        m, i = b // count, b % count
        hi, lo = split2(sum(other_ref[g, m, i : i + 1, :] for g in range(other_ref.shape[0])))
        in_row = in_row_ref[b]
        both = dot(jnp.concatenate([in_row * hi, in_row * lo], axis=0), cells_ref[b])
        inner.append(both[:side, :side] + (both[:side, side:] + both[side:, :side]))
    update = dot3(cosines_t_ref[...], jnp.concatenate(inner, axis=1))
    for b in range(3 * count):
        outs[b // count][b % count] = decoded_ref[b] + update[:, b * side : (b + 1) * side]


def call(kernel, out_shape, flops, *args, scratch=(), in_place={}):
    moved = sum(a.size * a.dtype.itemsize for a in args)
    specs = [
        pl.BlockSpec(memory_space=in_place.get(k, pltpu.VMEM)) for k in range(len(args))
    ]
    return pl.pallas_call(
        kernel,
        out_shape=out_shape,
        in_specs=specs,
        scratch_shapes=list(scratch),
        compiler_params=pltpu.CompilerParams(vmem_limit_bytes=24 * 1024 * 1024),
        cost_estimate=pl.CostEstimate(flops=flops, bytes_accessed=2 * moved, transcendentals=0),
    )(*args)


def ring_perms(count):
    chips = count // 2
    order = list(range(0, chips, 2)) + list(range(1, chips, 2))[::-1]
    forward = [
        (2 * order[p] + c, 2 * order[(p + 1) % chips] + c) for p in range(chips) for c in range(2)
    ]
    return forward, [(b, a) for a, b in forward], chips


def band_tables(band_index, side, ahead):
    blocks, keep = band_index.shape[0] * band_index.shape[1], band_index.shape[2]
    return call(
        tables_kernel,
        (
            jax.ShapeDtypeStruct((blocks, side, keep), BF16),
            jax.ShapeDtypeStruct((blocks, side, keep), BF16),
            jax.ShapeDtypeStruct((blocks, keep, side), BF16),
            jax.ShapeDtypeStruct((blocks, side, side), BF16),
        ),
        TABLES_FLOPS,
        band_index,
        ahead,
        in_place={1: pl.ANY},
    )


def column_moments(x, d, weights, momenta, band_index, cosines, cosines_t, shapes):
    side = weights[0].shape[1]
    rows, width = x.shape
    count = lax.axis_size("fsdp")
    swap = [(f, f ^ 1) for f in range(count)]
    forward, back, chips = ring_perms(count)

    def send(value, perm):
        return lax.ppermute(value, "fsdp", perm)

    xf, db, df, xb = send(x, forward), send(d, back), send(d, forward), send(x, back)
    xs, ds = [x, xf, xb], [d, df, db]
    partner_weights = [send(w, swap) for w in weights]
    pause = call(pause_kernel, jax.ShapeDtypeStruct((8, 128), F32), PAUSE_FLOPS)
    db, pause = lax.optimization_barrier((db, pause))
    arrived = []

    def with_weight(value):
        if len(arrived) == len(partner_weights):
            return value
        value, weight = lax.optimization_barrier((value, partner_weights[len(arrived)]))
        arrived.append(weight)
        return value

    for _ in range(chips // 2 - 2):
        db = with_weight(db)
        xf, db, df, xb = send(xf, forward), send(db, back), send(df, forward), send(xb, back)
        xs += [xf, xb]
        ds += [df, db]
    x_last, d_last = send(xf, forward), send(with_weight(db), back)
    partner_weights[: len(arrived)] = arrived

    def scratch(shards):
        return (
            pltpu.VMEM((shards * rows, width), BF16),
            pltpu.VMEM((shards * rows, width), BF16),
            pltpu.VMEM((6 * side, shards * rows), BF16),
        )

    part = jax.ShapeDtypeStruct((3, side, width), F32)
    early = len(xs) - 2
    own, partner, wgu, wd = call(
        functools.partial(early_kernel, early),
        (
            part,
            part,
            jax.ShapeDtypeStruct((4 * side, width), BF16),
            jax.ShapeDtypeStruct((2 * side, width), BF16),
        ),
        24 * early * rows * width * side,
        *xs[:early],
        *ds[:early],
        *weights,
        *partner_weights,
        pause,
        scratch=scratch(early),
    )
    own, partner = call(
        functools.partial(middle_kernel, 2),
        (part, part),
        24 * 2 * rows * width * side,
        *xs[early:],
        *ds[early:],
        wgu,
        wd,
        own,
        partner,
        scratch=scratch(2),
    )
    own_late, partner_late = call(
        late_kernel,
        (part, jax.ShapeDtypeStruct(part.shape, BF16)),
        LATE_FLOPS,
        x_last,
        d_last,
        wgu,
        wd,
    )
    in_row, in_col, in_col_t, mask = band_tables(band_index, side, own_late)
    moments = call(
        functools.partial(moment_kernel, 4),
        shapes,
        10**9,
        own,
        send(partner, swap),
        own_late,
        send(partner_late, swap),
        *momenta,
        in_row,
        in_col,
        mask,
        cosines,
        cosines_t,
    )
    return moments, in_row, in_col_t


def shared_column_moments(x, d, weights, momenta, band_index, cosines, cosines_t, shapes):
    gate_weight, up_weight, down_weight = weights
    own = shared_column_grads(x, d, gate_weight, up_weight, down_weight)
    in_row, in_col, in_col_t, mask = band_tables(band_index, cosines.shape[0], own)
    moments = call(
        functools.partial(moment_kernel, 1),
        shapes,
        0,
        own,
        *momenta,
        in_row,
        in_col,
        mask,
        cosines,
        cosines_t,
    )
    return moments, in_row, in_col_t


def shared_column_grads(x, d, gate_weight, up_weight, down_weight):
    side = gate_weight.shape[1]
    width = x.shape[1]
    blk_dev = gate_weight.shape[0]
    count = lax.axis_size("fsdp")
    share = width // side // blk_dev
    groups = [list(range(g * share, (g + 1) * share)) for g in range(count // share)]

    def whole(w):
        return lax.all_gather(w, "fsdp", axis=0, tiled=True, axis_index_groups=groups)

    gate, up = whole(gate_weight).reshape(width, side), whole(up_weight).reshape(width, side)
    down = whole(down_weight).transpose(1, 0, 2).reshape(side, width)
    x_all = lax.all_gather(x, "fsdp", axis=0, tiled=True)
    d_all = lax.all_gather(d, "fsdp", axis=0, tiled=True)
    gate_pre = jnp.dot(x_all, gate, preferred_element_type=F32)
    up_pre = jnp.dot(x_all, up, preferred_element_type=F32)
    d_hidden = jnp.dot(d_all, down.T, preferred_element_type=F32)
    sig = jax.nn.sigmoid(gate_pre)
    hidden = (gate_pre * sig * up_pre).astype(BF16)
    d_gate = (d_hidden * up_pre * sig * (1.0 + gate_pre * (1.0 - sig))).astype(BF16)
    d_up = (d_hidden * gate_pre * sig).astype(BF16)
    start = lax.rem(lax.axis_index("fsdp"), share) * blk_dev * side
    x_own = lax.dynamic_slice_in_dim(x_all, start, blk_dev * side, axis=1)
    d_own = lax.dynamic_slice_in_dim(d_all, start, blk_dev * side, axis=1)
    own = jnp.stack(
        [
            jnp.dot(d_gate.T, x_own, preferred_element_type=F32),
            jnp.dot(d_up.T, x_own, preferred_element_type=F32),
            jnp.dot(hidden.T, d_own, preferred_element_type=F32),
        ]
    )
    return own


def per_device(
    x_in, d_out, gate_weight, up_weight, down_weight, mom_gate, mom_up, mom_down, band_index
):
    side = gate_weight.shape[1]
    blk_dev = gate_weight.shape[0]
    row_blocks = x_in.shape[2] // side
    if blk_dev == row_blocks and lax.axis_size("fsdp") % 4 == 0:
        step = column_moments
    else:
        step = shared_column_moments
    cosines, cosines_t = jnp.asarray(dct_table(side)), jnp.asarray(dct_table(side).T)
    blocks = 3 * blk_dev
    dense = jax.ShapeDtypeStruct((blocks, side, side), F32)
    (moment, kept, band), in_row, in_col_t = step(
        x_in[0],
        d_out[0],
        (gate_weight, up_weight, down_weight),
        (mom_gate[0], mom_up[0], mom_down[0]),
        band_index,
        cosines,
        cosines_t,
        (dense, dense, jax.ShapeDtypeStruct(band_index.shape, F32)),
    )
    reps = lax.axis_size("rep")
    other = jnp.stack(
        [
            lax.ppermute(band, "rep", [(r, (r + s) % reps) for r in range(reps)])
            for s in range(1, reps)
        ]
    )
    result = jax.ShapeDtypeStruct((blk_dev, side, side), F32)
    flops = 4 * 3 * blocks * side**3
    *residuals, decoded, cells = call(
        residual_kernel,
        (result,) * 3 + (dense, jax.ShapeDtypeStruct((*in_col_t.shape[:2], 2 * side), BF16)),
        flops,
        moment,
        kept,
        in_col_t,
        cosines,
        cosines_t,
    )
    updates = call(
        update_kernel, (result,) * 3, flops, decoded, other, in_row, cells, cosines_t
    )
    return (*(r[None] for r in residuals), *updates)


def solution(mesh):
    in_specs = (
        P("rep", "fsdp", None),
        P("rep", "fsdp", None),
        P("fsdp", None, None),
        P("fsdp", None, None),
        P("fsdp", None, None),
        P("rep", "fsdp", None, None),
        P("rep", "fsdp", None, None),
        P("rep", "fsdp", None, None),
        P(None, "fsdp", None),
    )
    out_specs = (
        P("rep", "fsdp", None, None),
        P("rep", "fsdp", None, None),
        P("rep", "fsdp", None, None),
        P("fsdp", None, None),
        P("fsdp", None, None),
        P("fsdp", None, None),
    )
    return jax.shard_map(
        per_device, mesh=mesh, in_specs=in_specs, out_specs=out_specs, check_vma=False
    )
```

```python
import functools

import jax
import jax.numpy as jnp
import numpy as np
from jax import lax
from jax.experimental import pallas as pl
from jax.experimental.pallas import tpu as pltpu
from jax.sharding import PartitionSpec as P

MOMENTUM_DECAY = 0.999

TABLES_FLOPS = 10**10
PAUSE_FLOPS = 10**9
F32 = jnp.float32
BF16 = jnp.bfloat16


def dct_table(side):
    k = np.arange(side, dtype=np.float64)[:, None]
    n = np.arange(side, dtype=np.float64)[None, :]
    scale = np.where(k == 0, np.sqrt(1.0 / side), np.sqrt(2.0 / side))
    return (scale * np.cos(np.pi * (2.0 * n + 1.0) * k / (2.0 * side))).astype(np.float32)


def split2(value):
    hi = value.astype(BF16)
    return hi, (value - hi.astype(F32)).astype(BF16)


def dot(a, b):
    return jnp.dot(a, b, preferred_element_type=F32)


def dot_nt(a, b):
    return lax.dot_general(a, b, (((1,), (1,)), ((), ())), preferred_element_type=F32)


def dot3(a, b):
    a_hi, a_lo = split2(a)
    b_hi, b_lo = split2(b)
    left = jnp.concatenate([a_hi, a_hi, a_lo], axis=1)
    return dot(left, jnp.concatenate([b_hi, b_lo, b_hi], axis=0))


def lanes_to_rows(value, side):
    count = value.shape[1] // side
    return jnp.concatenate([value[:, i * side : (i + 1) * side] for i in range(count)], axis=0)


def activations(wgu, wd, x, d):
    pre = dot_nt(wgu, x)
    dh = dot_nt(wd, d)
    gate, up = pre[: wd.shape[0]], pre[wd.shape[0] :]
    sig = 1.0 / (1.0 + jnp.exp(-gate))
    swish = gate * sig
    d_gate = (dh * up * sig * (1.0 + gate * (1.0 - sig))).astype(BF16)
    return d_gate, (dh * swish).astype(BF16), (swish * up).astype(BF16)


def tables_kernel(index_ref, *refs):
    in_row_ref, in_col_ref, in_col_t_ref, mask_ref = refs[-4:]
    side = mask_ref.shape[1]
    shift = int(np.log2(side))
    matrices, count, keep = index_ref.shape
    lines = lax.broadcasted_iota(jnp.int32, (side, keep), 0)
    for m in range(matrices):
        for i in range(count):
            b = m * count + i
            index = index_ref[m, i : i + 1, :]
            in_row = jnp.where((index >> shift) == lines, 1.0, 0.0).astype(BF16)
            in_col = jnp.where((index & (side - 1)) == lines, 1.0, 0.0).astype(BF16)
            in_col_t = in_col.T
            in_row_ref[b] = in_row
            in_col_ref[b] = in_col
            in_col_t_ref[b] = in_col_t
            mask_ref[b] = dot(in_row, in_col_t).astype(BF16)


def pause_kernel(out_ref):
    out_ref[...] = jnp.zeros_like(out_ref)


def column_grads(xs, ds, wgu, wd, x_all, d_all, act):
    rows, half = xs[0].shape[0], wd.shape[0]
    for s in range(0, len(xs), 2):
        some = range(s, min(s + 2, len(xs)))
        x = jnp.concatenate([xs[j][...] for j in some], axis=0)
        d = jnp.concatenate([ds[j][...] for j in some], axis=0)
        span = pl.ds(s * rows, len(some) * rows)
        x_all[span, :] = x
        d_all[span, :] = d
        d_gate, d_up, hidden = activations(wgu, wd, x, d)
        act[:half, span] = d_gate
        act[half : 2 * half, span] = d_up
        act[2 * half :, span] = hidden
    g_in = dot(act[: 2 * half, :], x_all[...])
    return g_in[:half], g_in[half:], dot(act[2 * half :, :], d_all[...])


def early_kernel(shards, *refs):
    xs, ds, weights = refs[:shards], refs[shards : 2 * shards], refs[2 * shards : 2 * shards + 6]
    own_ref, par_ref, wgu_ref, wd_ref, *scratch = refs[2 * shards + 7 :]
    count, side, _ = weights[0].shape
    for i in range(count):
        cols = slice(i * side, (i + 1) * side)
        for p in range(2):
            gate, up, down = (ref[i] for ref in weights[3 * p : 3 * p + 3])
            wgu_ref[p * side : (p + 1) * side, cols] = gate.T
            wgu_ref[(2 + p) * side : (3 + p) * side, cols] = up.T
            wd_ref[p * side : (p + 1) * side, cols] = down
    for m, grad in enumerate(column_grads(xs, ds, wgu_ref[...], wd_ref[...], *scratch)):
        own_ref[m] = grad[:side]
        par_ref[m] = grad[side:]


def middle_kernel(shards, *refs):
    xs, ds = refs[:shards], refs[shards : 2 * shards]
    wgu_ref, wd_ref, own_in, par_in, own_ref, par_ref, *scratch = refs[2 * shards :]
    side = own_ref.shape[1]
    for m, grad in enumerate(column_grads(xs, ds, wgu_ref[...], wd_ref[...], *scratch)):
        own_ref[m] = own_in[m] + grad[:side]
        par_ref[m] = par_in[m] + grad[side:]


def moment_step(
    grads, mom_refs, in_row_ref, in_col_ref, mask_ref, cosines_ref, cosines_t_ref, moment_ref, kept_ref, band_ref
):
    side = cosines_ref.shape[0]
    count = mom_refs[0].shape[0]
    blocks = []
    for m in range(3):
        for i in range(count):
            piece = grads[m][:, i * side : (i + 1) * side]
            if m < 2:
                piece = piece.T
            block = MOMENTUM_DECAY * mom_refs[m][i] + piece
            moment_ref[m * count + i] = block
            blocks.append(block)
    inner = dot3(cosines_ref[...], jnp.concatenate(blocks, axis=1))
    coeffs = dot3(lanes_to_rows(inner, side), cosines_t_ref[...])
    for m in range(3):
        for i in range(count):
            b = m * count + i
            block = coeffs[b * side : (b + 1) * side]
            kept_ref[b] = block * mask_ref[b].astype(F32)
            hi, lo = split2(block)
            in_col = in_col_ref[b]
            at_col = dot(jnp.concatenate([hi, lo], axis=1), jnp.concatenate([in_col, in_col], axis=0))
            band_ref[m, i : i + 1, :] = jnp.sum(
                at_col * in_row_ref[b].astype(F32), axis=0, keepdims=True
            )


def late_kernel(*refs):
    xs, ds, wgu_ref, wd_ref, own_ref, got_ref = refs[:2], refs[2:4], *refs[4:8]
    side = own_ref.shape[1]
    x = jnp.concatenate([ref[...] for ref in xs], axis=0)
    d = jnp.concatenate([ref[...] for ref in ds], axis=0)
    wgu = jnp.concatenate([wgu_ref[:side, :], wgu_ref[2 * side : 3 * side, :]], axis=0)
    d_gate, d_up, hidden = activations(wgu, wd_ref[:side, :], x, d)
    late = (dot(d_gate, x), dot(d_up, x), dot(hidden, d))
    grads = [late[m] + (own_ref[m] + got_ref[m]) for m in range(3)]
    moment_step(grads, refs[8:11], *refs[11:])


def moment_kernel(grad_ref, *refs):
    moment_step([grad_ref[m] for m in range(3)], refs[:3], *refs[3:])


def residual_kernel(moment_ref, kept_ref, in_col_t_ref, cosines_ref, cosines_t_ref, *outs):
    *residuals, decoded_ref, cells_ref = outs
    side = cosines_ref.shape[0]
    count = residuals[0].shape[0]
    blocks = range(3 * count)
    cosines = cosines_ref[...]
    inner = dot3(jnp.concatenate([kept_ref[b] for b in blocks], axis=0), cosines)
    inner = jnp.concatenate([inner[b * side : (b + 1) * side] for b in blocks], axis=1)
    decoded = dot3(cosines_t_ref[...], inner)
    for b in blocks:
        kept = decoded[:, b * side : (b + 1) * side]
        decoded_ref[b] = kept
        residuals[b // count][b % count] = moment_ref[b] - kept
    parts = jnp.concatenate(split2(cosines), axis=1)
    for b in blocks:
        cells_ref[b] = dot(in_col_t_ref[b], parts).astype(BF16)


def update_kernel(decoded_ref, other_ref, in_row_ref, cells_ref, cosines_t_ref, *outs):
    side = cosines_t_ref.shape[0]
    count = outs[0].shape[0]
    inner = []
    for b in range(3 * count):
        m, i = b // count, b % count
        hi, lo = split2(sum(other_ref[g, m, i : i + 1, :] for g in range(other_ref.shape[0])))
        in_row = in_row_ref[b]
        both = dot(jnp.concatenate([in_row * hi, in_row * lo], axis=0), cells_ref[b])
        inner.append(both[:side, :side] + (both[:side, side:] + both[side:, :side]))
    update = dot3(cosines_t_ref[...], jnp.concatenate(inner, axis=1))
    for b in range(3 * count):
        outs[b // count][b % count] = decoded_ref[b] + update[:, b * side : (b + 1) * side]


def call(kernel, out_shape, flops, *args, scratch=(), in_place={}):
    moved = sum(a.size * a.dtype.itemsize for a in args)
    specs = [
        pl.BlockSpec(memory_space=in_place.get(k, pltpu.VMEM)) for k in range(len(args))
    ]
    return pl.pallas_call(
        kernel,
        out_shape=out_shape,
        in_specs=specs,
        scratch_shapes=list(scratch),
        compiler_params=pltpu.CompilerParams(vmem_limit_bytes=24 * 1024 * 1024),
        cost_estimate=pl.CostEstimate(flops=flops, bytes_accessed=2 * moved, transcendentals=0),
    )(*args)


def ring_perms(count):
    chips = count // 2
    order = list(range(0, chips, 2)) + list(range(1, chips, 2))[::-1]
    forward = [
        (2 * order[p] + c, 2 * order[(p + 1) % chips] + c) for p in range(chips) for c in range(2)
    ]
    return forward, [(b, a) for a, b in forward], chips


def band_tables(band_index, side, *ahead):
    blocks, keep = band_index.shape[0] * band_index.shape[1], band_index.shape[2]
    return call(
        tables_kernel,
        (
            jax.ShapeDtypeStruct((blocks, side, keep), BF16),
            jax.ShapeDtypeStruct((blocks, side, keep), BF16),
            jax.ShapeDtypeStruct((blocks, keep, side), BF16),
            jax.ShapeDtypeStruct((blocks, side, side), BF16),
        ),
        TABLES_FLOPS,
        band_index,
        *ahead,
        in_place=dict.fromkeys(range(1, 1 + len(ahead)), pl.ANY),
    )


def column_moments(x, d, weights, momenta, band_index, cosines, cosines_t, shapes):
    side = weights[0].shape[1]
    rows, width = x.shape
    count = lax.axis_size("fsdp")
    swap = [(f, f ^ 1) for f in range(count)]
    forward, back, chips = ring_perms(count)

    def send(value, perm):
        return lax.ppermute(value, "fsdp", perm)

    xf, db, df, xb = send(x, forward), send(d, back), send(d, forward), send(x, back)
    xs, ds = [x, xf, xb], [d, df, db]
    partner_weights = [send(w, swap) for w in weights]
    pause = call(pause_kernel, jax.ShapeDtypeStruct((8, 128), F32), PAUSE_FLOPS)
    db, pause = lax.optimization_barrier((db, pause))
    arrived = []

    def with_weight(value):
        if len(arrived) == len(partner_weights):
            return value
        value, weight = lax.optimization_barrier((value, partner_weights[len(arrived)]))
        arrived.append(weight)
        return value

    for _ in range(chips // 2 - 2):
        db = with_weight(db)
        xf, db, df, xb = send(xf, forward), send(db, back), send(df, forward), send(xb, back)
        xs += [xf, xb]
        ds += [df, db]
    x_last, d_last = send(xf, forward), send(with_weight(db), back)
    partner_weights[: len(arrived)] = arrived

    def scratch(shards):
        return (
            pltpu.VMEM((shards * rows, width), BF16),
            pltpu.VMEM((shards * rows, width), BF16),
            pltpu.VMEM((6 * side, shards * rows), BF16),
        )

    part = jax.ShapeDtypeStruct((3, side, width), F32)
    early = len(xs) - 2
    own, partner, wgu, wd = call(
        functools.partial(early_kernel, early),
        (
            part,
            part,
            jax.ShapeDtypeStruct((4 * side, width), BF16),
            jax.ShapeDtypeStruct((2 * side, width), BF16),
        ),
        24 * early * rows * width * side,
        *xs[:early],
        *ds[:early],
        *weights,
        *partner_weights,
        pause,
        scratch=scratch(early),
    )
    own, partner = call(
        functools.partial(middle_kernel, 2),
        (part, part),
        24 * 2 * rows * width * side,
        *xs[early:],
        *ds[early:],
        wgu,
        wd,
        own,
        partner,
        scratch=scratch(2),
    )
    got = send(partner, swap)
    x_swap, d_swap = send(x_last, swap), send(d_last, swap)
    in_row, in_col, in_col_t, mask = band_tables(band_index, side, x_last, d_last)
    moments = call(
        late_kernel,
        shapes,
        10**9,
        x_last,
        x_swap,
        d_last,
        d_swap,
        wgu,
        wd,
        own,
        got,
        *momenta,
        in_row,
        in_col,
        mask,
        cosines,
        cosines_t,
    )
    return moments, in_row, in_col_t


def shared_column_moments(x, d, weights, momenta, band_index, cosines, cosines_t, shapes):
    gate_weight, up_weight, down_weight = weights
    own = shared_column_grads(x, d, gate_weight, up_weight, down_weight)
    in_row, in_col, in_col_t, mask = band_tables(band_index, cosines.shape[0], own)
    moments = call(
        moment_kernel,
        shapes,
        0,
        own,
        *momenta,
        in_row,
        in_col,
        mask,
        cosines,
        cosines_t,
    )
    return moments, in_row, in_col_t


def shared_column_grads(x, d, gate_weight, up_weight, down_weight):
    side = gate_weight.shape[1]
    width = x.shape[1]
    blk_dev = gate_weight.shape[0]
    count = lax.axis_size("fsdp")
    share = width // side // blk_dev
    groups = [list(range(g * share, (g + 1) * share)) for g in range(count // share)]

    def whole(w):
        return lax.all_gather(w, "fsdp", axis=0, tiled=True, axis_index_groups=groups)

    gate, up = whole(gate_weight).reshape(width, side), whole(up_weight).reshape(width, side)
    down = whole(down_weight).transpose(1, 0, 2).reshape(side, width)
    x_all = lax.all_gather(x, "fsdp", axis=0, tiled=True)
    d_all = lax.all_gather(d, "fsdp", axis=0, tiled=True)
    gate_pre = jnp.dot(x_all, gate, preferred_element_type=F32)
    up_pre = jnp.dot(x_all, up, preferred_element_type=F32)
    d_hidden = jnp.dot(d_all, down.T, preferred_element_type=F32)
    sig = jax.nn.sigmoid(gate_pre)
    hidden = (gate_pre * sig * up_pre).astype(BF16)
    d_gate = (d_hidden * up_pre * sig * (1.0 + gate_pre * (1.0 - sig))).astype(BF16)
    d_up = (d_hidden * gate_pre * sig).astype(BF16)
    start = lax.rem(lax.axis_index("fsdp"), share) * blk_dev * side
    x_own = lax.dynamic_slice_in_dim(x_all, start, blk_dev * side, axis=1)
    d_own = lax.dynamic_slice_in_dim(d_all, start, blk_dev * side, axis=1)
    own = jnp.stack(
        [
            jnp.dot(d_gate.T, x_own, preferred_element_type=F32),
            jnp.dot(d_up.T, x_own, preferred_element_type=F32),
            jnp.dot(hidden.T, d_own, preferred_element_type=F32),
        ]
    )
    return own


def per_device(
    x_in, d_out, gate_weight, up_weight, down_weight, mom_gate, mom_up, mom_down, band_index
):
    side = gate_weight.shape[1]
    blk_dev = gate_weight.shape[0]
    row_blocks = x_in.shape[2] // side
    if blk_dev == row_blocks and lax.axis_size("fsdp") % 4 == 0:
        step = column_moments
    else:
        step = shared_column_moments
    cosines, cosines_t = jnp.asarray(dct_table(side)), jnp.asarray(dct_table(side).T)
    blocks = 3 * blk_dev
    dense = jax.ShapeDtypeStruct((blocks, side, side), F32)
    (moment, kept, band), in_row, in_col_t = step(
        x_in[0],
        d_out[0],
        (gate_weight, up_weight, down_weight),
        (mom_gate[0], mom_up[0], mom_down[0]),
        band_index,
        cosines,
        cosines_t,
        (dense, dense, jax.ShapeDtypeStruct(band_index.shape, F32)),
    )
    reps = lax.axis_size("rep")
    other = jnp.stack(
        [
            lax.ppermute(band, "rep", [(r, (r + s) % reps) for r in range(reps)])
            for s in range(1, reps)
        ]
    )
    result = jax.ShapeDtypeStruct((blk_dev, side, side), F32)
    flops = 4 * 3 * blocks * side**3
    *residuals, decoded, cells = call(
        residual_kernel,
        (result,) * 3 + (dense, jax.ShapeDtypeStruct((*in_col_t.shape[:2], 2 * side), BF16)),
        flops,
        moment,
        kept,
        in_col_t,
        cosines,
        cosines_t,
    )
    updates = call(
        update_kernel, (result,) * 3, flops, decoded, other, in_row, cells, cosines_t
    )
    return (*(r[None] for r in residuals), *updates)


def solution(mesh):
    in_specs = (
        P("rep", "fsdp", None),
        P("rep", "fsdp", None),
        P("fsdp", None, None),
        P("fsdp", None, None),
        P("fsdp", None, None),
        P("rep", "fsdp", None, None),
        P("rep", "fsdp", None, None),
        P("rep", "fsdp", None, None),
        P(None, "fsdp", None),
    )
    out_specs = (
        P("rep", "fsdp", None, None),
        P("rep", "fsdp", None, None),
        P("rep", "fsdp", None, None),
        P("fsdp", None, None),
        P("fsdp", None, None),
        P("fsdp", None, None),
    )
    return jax.shard_map(
        per_device, mesh=mesh, in_specs=in_specs, out_specs=out_specs, check_vma=False
    )
```

```python
import functools

import jax
import jax.numpy as jnp
import numpy as np
from jax import lax
from jax.experimental import pallas as pl
from jax.experimental.pallas import tpu as pltpu
from jax.sharding import PartitionSpec as P

MOMENTUM_DECAY = 0.999

TABLES_FLOPS = 10**9
LAST_FLOPS = 10**10
PAUSE_FLOPS = 10**9
F32 = jnp.float32
BF16 = jnp.bfloat16


def dct_table(side):
    k = np.arange(side, dtype=np.float64)[:, None]
    n = np.arange(side, dtype=np.float64)[None, :]
    scale = np.where(k == 0, np.sqrt(1.0 / side), np.sqrt(2.0 / side))
    return (scale * np.cos(np.pi * (2.0 * n + 1.0) * k / (2.0 * side))).astype(np.float32)


def split2(value):
    hi = value.astype(BF16)
    return hi, (value - hi.astype(F32)).astype(BF16)


def dot(a, b):
    return jnp.dot(a, b, preferred_element_type=F32)


def dot_nt(a, b):
    return lax.dot_general(a, b, (((1,), (1,)), ((), ())), preferred_element_type=F32)


def dot3(a, b):
    a_hi, a_lo = split2(a)
    b_hi, b_lo = split2(b)
    left = jnp.concatenate([a_hi, a_hi, a_lo], axis=1)
    return dot(left, jnp.concatenate([b_hi, b_lo, b_hi], axis=0))


def lanes_to_rows(value, side):
    count = value.shape[1] // side
    return jnp.concatenate([value[:, i * side : (i + 1) * side] for i in range(count)], axis=0)


def activations(wgu, wd, x, d):
    pre = dot_nt(wgu, x)
    dh = dot_nt(wd, d)
    gate, up = pre[: wd.shape[0]], pre[wd.shape[0] :]
    sig = 1.0 / (1.0 + jnp.exp(-gate))
    swish = gate * sig
    d_gate = (dh * up * sig * (1.0 + gate * (1.0 - sig))).astype(BF16)
    return d_gate, (dh * swish).astype(BF16), (swish * up).astype(BF16)


def tables_kernel(index_ref, *refs):
    in_row_ref, in_col_ref, in_col_t_ref, mask_ref = refs[-4:]
    side = mask_ref.shape[1]
    shift = int(np.log2(side))
    matrices, count, keep = index_ref.shape
    lines = lax.broadcasted_iota(jnp.int32, (side, keep), 0)
    for m in range(matrices):
        for i in range(count):
            b = m * count + i
            index = index_ref[m, i : i + 1, :]
            in_row = jnp.where((index >> shift) == lines, 1.0, 0.0).astype(BF16)
            in_col = jnp.where((index & (side - 1)) == lines, 1.0, 0.0).astype(BF16)
            in_col_t = in_col.T
            in_row_ref[b] = in_row
            in_col_ref[b] = in_col
            in_col_t_ref[b] = in_col_t
            mask_ref[b] = dot(in_row, in_col_t).astype(BF16)


def pause_kernel(*refs):
    refs[-1][...] = jnp.zeros_like(refs[-1])


def pause(flops, *ahead):
    return call(
        pause_kernel,
        jax.ShapeDtypeStruct((8, 128), F32),
        flops,
        *ahead,
        in_place=dict.fromkeys(range(len(ahead)), pl.ANY),
    )


def column_grads(xs, ds, wgu, wd, x_all, d_all, act):
    rows, half = xs[0].shape[0], wd.shape[0]
    for s in range(0, len(xs), 2):
        some = range(s, min(s + 2, len(xs)))
        x = jnp.concatenate([xs[j][...] for j in some], axis=0)
        d = jnp.concatenate([ds[j][...] for j in some], axis=0)
        span = pl.ds(s * rows, len(some) * rows)
        x_all[span, :] = x
        d_all[span, :] = d
        d_gate, d_up, hidden = activations(wgu, wd, x, d)
        act[:half, span] = d_gate
        act[half : 2 * half, span] = d_up
        act[2 * half :, span] = hidden
    g_in = dot(act[: 2 * half, :], x_all[...])
    return g_in[:half], g_in[half:], dot(act[2 * half :, :], d_all[...])


def early_kernel(shards, *refs):
    xs, ds, weights = refs[:shards], refs[shards : 2 * shards], refs[2 * shards : 2 * shards + 6]
    own_ref, par_ref, wgu_ref, wd_ref, *scratch = refs[2 * shards + 7 :]
    count, side, _ = weights[0].shape
    for i in range(count):
        cols = slice(i * side, (i + 1) * side)
        for p in range(2):
            gate, up, down = (ref[i] for ref in weights[3 * p : 3 * p + 3])
            wgu_ref[p * side : (p + 1) * side, cols] = gate.T
            wgu_ref[(2 + p) * side : (3 + p) * side, cols] = up.T
            wd_ref[p * side : (p + 1) * side, cols] = down
    for m, grad in enumerate(column_grads(xs, ds, wgu_ref[...], wd_ref[...], *scratch)):
        own_ref[m] = grad[:side]
        par_ref[m] = grad[side:]


def middle_kernel(shards, *refs):
    xs, ds = refs[:shards], refs[shards : 2 * shards]
    wgu_ref, wd_ref, own_in, par_in, own_ref, par_ref, *scratch = refs[2 * shards :]
    side = own_ref.shape[1]
    for m, grad in enumerate(column_grads(xs, ds, wgu_ref[...], wd_ref[...], *scratch)):
        own_ref[m] = own_in[m] + grad[:side]
        par_ref[m] = par_in[m] + grad[side:]


def block_of(grads, m, i, side):
    piece = grads[m][:, i * side : (i + 1) * side]
    return piece.T if m < 2 else piece


def moment_step(blocks, in_row_ref, in_col_ref, mask_ref, cosines_ref, cosines_t_ref, moment_ref, kept_ref, band_ref):
    side = cosines_ref.shape[0]
    count = len(blocks) // 3
    for b, block in enumerate(blocks):
        moment_ref[b] = block
    inner = dot3(cosines_ref[...], jnp.concatenate(blocks, axis=1))
    coeffs = dot3(lanes_to_rows(inner, side), cosines_t_ref[...])
    for m in range(3):
        for i in range(count):
            b = m * count + i
            block = coeffs[b * side : (b + 1) * side]
            kept_ref[b] = block * mask_ref[b].astype(F32)
            hi, lo = split2(block)
            in_col = in_col_ref[b]
            at_col = dot(jnp.concatenate([hi, lo], axis=1), jnp.concatenate([in_col, in_col], axis=0))
            band_ref[m, i : i + 1, :] = jnp.sum(
                at_col * in_row_ref[b].astype(F32), axis=0, keepdims=True
            )


def late_grads(x_ref, d_ref, wgu_ref, wd_ref, add_ref):
    side = add_ref.shape[1]
    x, d = x_ref[...], d_ref[...]
    wgu = jnp.concatenate([wgu_ref[:side, :], wgu_ref[2 * side : 3 * side, :]], axis=0)
    d_gate, d_up, hidden = activations(wgu, wd_ref[:side, :], x, d)
    return [add_ref[m] + late for m, late in enumerate((dot(d_gate, x), dot(d_up, x), dot(hidden, d)))]


def base_kernel(x_ref, d_ref, wgu_ref, wd_ref, own_ref, mg_ref, mu_ref, md_ref, base_ref):
    grads = late_grads(x_ref, d_ref, wgu_ref, wd_ref, own_ref)
    count, side, _ = mg_ref.shape
    for m, mom_ref in enumerate((mg_ref, mu_ref, md_ref)):
        for i in range(count):
            base_ref[m * count + i] = MOMENTUM_DECAY * mom_ref[i] + block_of(grads, m, i, side)


def late_kernel(_, x_ref, d_ref, wgu_ref, wd_ref, got_ref, base_ref, *refs):
    grads = late_grads(x_ref, d_ref, wgu_ref, wd_ref, got_ref)
    blocks, side, _ = base_ref.shape
    count = blocks // 3
    moment_step(
        [base_ref[b] + block_of(grads, b // count, b % count, side) for b in range(blocks)], *refs
    )


def moment_kernel(grad_ref, mg_ref, mu_ref, md_ref, *refs):
    count, side, _ = mg_ref.shape
    grads = [grad_ref[m] for m in range(3)]
    moment_step(
        [
            MOMENTUM_DECAY * mom_ref[i] + block_of(grads, m, i, side)
            for m, mom_ref in enumerate((mg_ref, mu_ref, md_ref))
            for i in range(count)
        ],
        *refs,
    )


def residual_kernel(moment_ref, kept_ref, in_col_t_ref, cosines_ref, cosines_t_ref, *outs):
    *residuals, decoded_ref, cells_ref = outs
    side = cosines_ref.shape[0]
    count = residuals[0].shape[0]
    blocks = range(3 * count)
    cosines = cosines_ref[...]
    inner = dot3(jnp.concatenate([kept_ref[b] for b in blocks], axis=0), cosines)
    inner = jnp.concatenate([inner[b * side : (b + 1) * side] for b in blocks], axis=1)
    decoded = dot3(cosines_t_ref[...], inner)
    for b in blocks:
        kept = decoded[:, b * side : (b + 1) * side]
        decoded_ref[b] = kept
        residuals[b // count][b % count] = moment_ref[b] - kept
    parts = jnp.concatenate(split2(cosines), axis=1)
    for b in blocks:
        cells_ref[b] = dot(in_col_t_ref[b], parts).astype(BF16)


def update_kernel(decoded_ref, other_ref, in_row_ref, cells_ref, cosines_t_ref, *refs):
    outs, (held, sems) = refs[:3], refs[3:]
    side = cosines_t_ref.shape[0]
    count = held.shape[1]
    copies = [pltpu.make_async_copy(held.at[m], outs[m], sems.at[m]) for m in range(3)]
    inner = []
    for b in range(3 * count):
        m, i = b // count, b % count
        hi, lo = split2(sum(other_ref[g, m, i : i + 1, :] for g in range(other_ref.shape[0])))
        in_row = in_row_ref[b]
        both = dot(jnp.concatenate([in_row * hi, in_row * lo], axis=0), cells_ref[b])
        inner.append(both[:side, :side] + (both[:side, side:] + both[side:, :side]))
    for m in range(3):
        update = dot3(cosines_t_ref[...], jnp.concatenate(inner[m * count : (m + 1) * count], axis=1))
        for i in range(count):
            held[m, i] = decoded_ref[m * count + i] + update[:, i * side : (i + 1) * side]
        copies[m].start()
    for copy in copies:
        copy.wait()


def call(kernel, out_shape, flops, *args, scratch=(), in_place={}, out_specs=None):
    moved = sum(a.size * a.dtype.itemsize for a in args)
    specs = [
        pl.BlockSpec(memory_space=in_place.get(k, pltpu.VMEM)) for k in range(len(args))
    ]
    return pl.pallas_call(
        kernel,
        out_shape=out_shape,
        in_specs=specs,
        **({} if out_specs is None else {"out_specs": out_specs}),
        scratch_shapes=list(scratch),
        compiler_params=pltpu.CompilerParams(vmem_limit_bytes=24 * 1024 * 1024),
        cost_estimate=pl.CostEstimate(flops=flops, bytes_accessed=2 * moved, transcendentals=0),
    )(*args)


def ring_perms(count):
    chips = count // 2
    order = list(range(0, chips, 2)) + list(range(1, chips, 2))[::-1]
    forward = [
        (2 * order[p] + c, 2 * order[(p + 1) % chips] + c) for p in range(chips) for c in range(2)
    ]
    return forward, [(b, a) for a, b in forward], chips


def band_tables(band_index, side, *ahead):
    blocks, keep = band_index.shape[0] * band_index.shape[1], band_index.shape[2]
    return call(
        tables_kernel,
        (
            jax.ShapeDtypeStruct((blocks, side, keep), BF16),
            jax.ShapeDtypeStruct((blocks, side, keep), BF16),
            jax.ShapeDtypeStruct((blocks, keep, side), BF16),
            jax.ShapeDtypeStruct((blocks, side, side), BF16),
        ),
        TABLES_FLOPS,
        band_index,
        *ahead,
        in_place=dict.fromkeys(range(1, 1 + len(ahead)), pl.ANY),
    )


def column_moments(x, d, weights, momenta, band_index, cosines, cosines_t, shapes):
    side = weights[0].shape[1]
    rows, width = x.shape
    count = lax.axis_size("fsdp")
    swap = [(f, f ^ 1) for f in range(count)]
    forward, back, chips = ring_perms(count)

    def send(value, perm):
        return lax.ppermute(value, "fsdp", perm)

    xf, db, df, xb = send(x, forward), send(d, back), send(d, forward), send(x, back)
    xs, ds = [x, xf, xb], [d, df, db]
    partner_weights = [send(w, swap) for w in weights]
    work = pause(PAUSE_FLOPS)
    db, work = lax.optimization_barrier((db, work))
    arrived = []

    def with_weight(value):
        if len(arrived) == len(partner_weights):
            return value
        value, weight = lax.optimization_barrier((value, partner_weights[len(arrived)]))
        arrived.append(weight)
        return value

    for _ in range(chips // 2 - 2):
        db = with_weight(db)
        xf, db, df, xb = send(xf, forward), send(db, back), send(df, forward), send(xb, back)
        xs += [xf, xb]
        ds += [df, db]
    x_last, d_last = send(xf, forward), send(with_weight(db), back)
    partner_weights[: len(arrived)] = arrived

    def scratch(shards):
        return (
            pltpu.VMEM((shards * rows, width), BF16),
            pltpu.VMEM((shards * rows, width), BF16),
            pltpu.VMEM((6 * side, shards * rows), BF16),
        )

    part = jax.ShapeDtypeStruct((3, side, width), F32)
    early = len(xs) - 2
    own, partner, wgu, wd = call(
        functools.partial(early_kernel, early),
        (
            part,
            part,
            jax.ShapeDtypeStruct((4 * side, width), BF16),
            jax.ShapeDtypeStruct((2 * side, width), BF16),
        ),
        24 * early * rows * width * side,
        *xs[:early],
        *ds[:early],
        *weights,
        *partner_weights,
        work,
        scratch=scratch(early),
    )
    own, partner = call(
        functools.partial(middle_kernel, 2),
        (part, part),
        24 * 2 * rows * width * side,
        *xs[early:],
        *ds[early:],
        wgu,
        wd,
        own,
        partner,
        scratch=scratch(2),
    )
    got = send(partner, swap)
    x_swap, d_swap = send(x_last, swap), send(d_last, swap)
    in_row, in_col, in_col_t, mask = band_tables(band_index, side, partner)
    late_flops = 24 * rows * width * side
    base = call(
        base_kernel, shapes[0], late_flops, x_last, d_last, wgu, wd, own, *momenta
    )
    moments = call(
        late_kernel,
        shapes,
        late_flops,
        pause(LAST_FLOPS, x_last, d_last),
        x_swap,
        d_swap,
        wgu,
        wd,
        got,
        base,
        in_row,
        in_col,
        mask,
        cosines,
        cosines_t,
    )
    return moments, in_row, in_col_t


def shared_column_moments(x, d, weights, momenta, band_index, cosines, cosines_t, shapes):
    gate_weight, up_weight, down_weight = weights
    own = shared_column_grads(x, d, gate_weight, up_weight, down_weight)
    in_row, in_col, in_col_t, mask = band_tables(band_index, cosines.shape[0], own)
    moments = call(
        moment_kernel,
        shapes,
        0,
        own,
        *momenta,
        in_row,
        in_col,
        mask,
        cosines,
        cosines_t,
    )
    return moments, in_row, in_col_t


def shared_column_grads(x, d, gate_weight, up_weight, down_weight):
    side = gate_weight.shape[1]
    width = x.shape[1]
    blk_dev = gate_weight.shape[0]
    count = lax.axis_size("fsdp")
    share = width // side // blk_dev
    groups = [list(range(g * share, (g + 1) * share)) for g in range(count // share)]

    def whole(w):
        return lax.all_gather(w, "fsdp", axis=0, tiled=True, axis_index_groups=groups)

    gate, up = whole(gate_weight).reshape(width, side), whole(up_weight).reshape(width, side)
    down = whole(down_weight).transpose(1, 0, 2).reshape(side, width)
    x_all = lax.all_gather(x, "fsdp", axis=0, tiled=True)
    d_all = lax.all_gather(d, "fsdp", axis=0, tiled=True)
    gate_pre = jnp.dot(x_all, gate, preferred_element_type=F32)
    up_pre = jnp.dot(x_all, up, preferred_element_type=F32)
    d_hidden = jnp.dot(d_all, down.T, preferred_element_type=F32)
    sig = jax.nn.sigmoid(gate_pre)
    hidden = (gate_pre * sig * up_pre).astype(BF16)
    d_gate = (d_hidden * up_pre * sig * (1.0 + gate_pre * (1.0 - sig))).astype(BF16)
    d_up = (d_hidden * gate_pre * sig).astype(BF16)
    start = lax.rem(lax.axis_index("fsdp"), share) * blk_dev * side
    x_own = lax.dynamic_slice_in_dim(x_all, start, blk_dev * side, axis=1)
    d_own = lax.dynamic_slice_in_dim(d_all, start, blk_dev * side, axis=1)
    own = jnp.stack(
        [
            jnp.dot(d_gate.T, x_own, preferred_element_type=F32),
            jnp.dot(d_up.T, x_own, preferred_element_type=F32),
            jnp.dot(hidden.T, d_own, preferred_element_type=F32),
        ]
    )
    return own


def per_device(
    x_in, d_out, gate_weight, up_weight, down_weight, mom_gate, mom_up, mom_down, band_index
):
    side = gate_weight.shape[1]
    blk_dev = gate_weight.shape[0]
    row_blocks = x_in.shape[2] // side
    if blk_dev == row_blocks and lax.axis_size("fsdp") % 4 == 0:
        step = column_moments
    else:
        step = shared_column_moments
    cosines, cosines_t = jnp.asarray(dct_table(side)), jnp.asarray(dct_table(side).T)
    blocks = 3 * blk_dev
    dense = jax.ShapeDtypeStruct((blocks, side, side), F32)
    (moment, kept, band), in_row, in_col_t = step(
        x_in[0],
        d_out[0],
        (gate_weight, up_weight, down_weight),
        (mom_gate[0], mom_up[0], mom_down[0]),
        band_index,
        cosines,
        cosines_t,
        (dense, dense, jax.ShapeDtypeStruct(band_index.shape, F32)),
    )
    reps = lax.axis_size("rep")
    other = jnp.stack(
        [
            lax.ppermute(band, "rep", [(r, (r + s) % reps) for r in range(reps)])
            for s in range(1, reps)
        ]
    )
    result = jax.ShapeDtypeStruct((blk_dev, side, side), F32)
    flops = 4 * 3 * blocks * side**3
    *residuals, decoded, cells = call(
        residual_kernel,
        (result,) * 3 + (dense, jax.ShapeDtypeStruct((*in_col_t.shape[:2], 2 * side), BF16)),
        flops,
        moment,
        kept,
        in_col_t,
        cosines,
        cosines_t,
    )
    updates = call(
        update_kernel,
        (result,) * 3,
        flops,
        decoded,
        other,
        in_row,
        cells,
        cosines_t,
        scratch=(pltpu.VMEM((3, *result.shape), F32), pltpu.SemaphoreType.DMA((3,))),
        out_specs=[pl.BlockSpec(memory_space=pl.ANY)] * 3,
    )
    return (*(r[None] for r in residuals), *updates)


def solution(mesh):
    in_specs = (
        P("rep", "fsdp", None),
        P("rep", "fsdp", None),
        P("fsdp", None, None),
        P("fsdp", None, None),
        P("fsdp", None, None),
        P("rep", "fsdp", None, None),
        P("rep", "fsdp", None, None),
        P("rep", "fsdp", None, None),
        P(None, "fsdp", None),
    )
    out_specs = (
        P("rep", "fsdp", None, None),
        P("rep", "fsdp", None, None),
        P("rep", "fsdp", None, None),
        P("fsdp", None, None),
        P("fsdp", None, None),
        P("fsdp", None, None),
    )
    return jax.shard_map(
        per_device, mesh=mesh, in_specs=in_specs, out_specs=out_specs, check_vma=False
    )
```

```python
import functools

import jax
import jax.numpy as jnp
import numpy as np
from jax import lax
from jax.experimental import pallas as pl
from jax.experimental.pallas import tpu as pltpu
from jax.sharding import PartitionSpec as P

MOMENTUM_DECAY = 0.999
TABLES_FLOPS = 10**10
COLUMNS_FLOPS = 10**9
PAUSE_FLOPS = 10**9
F32 = jnp.float32
BF16 = jnp.bfloat16


def dct_table(side):
    k = np.arange(side, dtype=np.float64)[:, None]
    n = np.arange(side, dtype=np.float64)[None, :]
    scale = np.where(k == 0, np.sqrt(1.0 / side), np.sqrt(2.0 / side))
    return (scale * np.cos(np.pi * (2.0 * n + 1.0) * k / (2.0 * side))).astype(np.float32)


def split2(value):
    hi = value.astype(BF16)
    return hi, (value - hi.astype(F32)).astype(BF16)


def dot(a, b):
    return jnp.dot(a, b, preferred_element_type=F32)


def dot_nt(a, b):
    return lax.dot_general(a, b, (((1,), (1,)), ((), ())), preferred_element_type=F32)


def dot3(a, b):
    a_hi, a_lo = split2(a)
    b_hi, b_lo = split2(b)
    left = jnp.concatenate([a_hi, a_hi, a_lo], axis=1)
    return dot(left, jnp.concatenate([b_hi, b_lo, b_hi], axis=0))


def lanes_to_rows(value, side):
    count = value.shape[1] // side
    return jnp.concatenate([value[:, i * side : (i + 1) * side] for i in range(count)], axis=0)


def activations(wgu, wd, x, d):
    pre = dot_nt(wgu, x)
    dh = dot_nt(wd, d)
    gate, up = pre[: wd.shape[0]], pre[wd.shape[0] :]
    sig = jax.nn.sigmoid(gate)
    swish = gate * sig
    d_gate = (dh * up * sig * (1.0 + gate * (1.0 - sig))).astype(BF16)
    return d_gate, (dh * swish).astype(BF16), (swish * up).astype(BF16)


def one_hot(numbers, lines):
    return jnp.where(numbers == lines, 1.0, 0.0).astype(BF16)


def tables_kernel(index_ref, *refs):
    in_row_ref, in_col_ref = refs[-2:]
    blocks, side, keep = in_row_ref.shape
    count = index_ref.shape[1]
    shift = int(np.log2(side))
    lines = lax.broadcasted_iota(jnp.int32, (side, keep), 0)
    for b in range(blocks):
        index = index_ref[b // count, b % count : b % count + 1, :]
        in_row_ref[b] = one_hot(index >> shift, lines)
        in_col_ref[b] = one_hot(index & (side - 1), lines)


def columns_kernel(index_ref, *refs):
    out_ref = refs[-1]
    blocks, keep, side = out_ref.shape
    count = index_ref.shape[1]
    lines = lax.broadcasted_iota(jnp.int32, (side, keep), 0)
    for b in range(blocks):
        index = index_ref[b // count, b % count : b % count + 1, :]
        out_ref[b] = one_hot(index & (side - 1), lines).T


def pause_kernel(out_ref):
    out_ref[...] = jnp.zeros_like(out_ref)


def column_grads(xs, ds, wgu, wd, x_all, d_all, act):
    rows, half = xs[0].shape[0], wd.shape[0]
    for s in range(0, len(xs), 2):
        some = range(s, min(s + 2, len(xs)))
        x = jnp.concatenate([xs[j][...] for j in some], axis=0)
        d = jnp.concatenate([ds[j][...] for j in some], axis=0)
        span = pl.ds(s * rows, len(some) * rows)
        x_all[span, :] = x
        d_all[span, :] = d
        d_gate, d_up, hidden = activations(wgu, wd, x, d)
        act[:half, span] = d_gate
        act[half : 2 * half, span] = d_up
        act[2 * half :, span] = hidden
    g_in = dot(act[: 2 * half, :], x_all[...])
    return g_in[:half], g_in[half:], dot(act[2 * half :, :], d_all[...])


def early_kernel(shards, *refs):
    xs, ds, weights = refs[:shards], refs[shards : 2 * shards], refs[2 * shards : 2 * shards + 6]
    own_ref, par_ref, wgu_ref, wd_ref, *scratch = refs[2 * shards + 7 :]
    count, side, _ = weights[0].shape
    for i in range(count):
        cols = slice(i * side, (i + 1) * side)
        for p in range(2):
            gate, up, down = (ref[i] for ref in weights[3 * p : 3 * p + 3])
            wgu_ref[p * side : (p + 1) * side, cols] = gate.T
            wgu_ref[(2 + p) * side : (3 + p) * side, cols] = up.T
            wd_ref[p * side : (p + 1) * side, cols] = down
    for m, grad in enumerate(column_grads(xs, ds, wgu_ref[...], wd_ref[...], *scratch)):
        own_ref[m] = grad[:side]
        par_ref[m] = grad[side:]


def middle_kernel(shards, *refs):
    xs, ds = refs[:shards], refs[shards : 2 * shards]
    wgu_ref, wd_ref, own_in, par_in, own_ref, par_ref, *scratch = refs[2 * shards :]
    side = own_ref.shape[1]
    for m, grad in enumerate(column_grads(xs, ds, wgu_ref[...], wd_ref[...], *scratch)):
        own_ref[m] = own_in[m] + grad[:side]
        par_ref[m] = par_in[m] + grad[side:]


def moment_step(
    grads, mom_refs, in_row_ref, in_col_ref, cosines_ref, cosines_t_ref, moment_ref, coeffs_ref, band_ref
):
    side = cosines_ref.shape[0]
    count = mom_refs[0].shape[0]
    blocks = []
    for m in range(3):
        for i in range(count):
            piece = grads[m][:, i * side : (i + 1) * side]
            if m < 2:
                piece = piece.T
            block = MOMENTUM_DECAY * mom_refs[m][i] + piece
            moment_ref[m * count + i] = block
            blocks.append(block)
    inner = dot3(cosines_ref[...], jnp.concatenate(blocks, axis=1))
    coeffs = dot3(lanes_to_rows(inner, side), cosines_t_ref[...])
    for m in range(3):
        for i in range(count):
            b = m * count + i
            block = coeffs[b * side : (b + 1) * side]
            coeffs_ref[b] = block
            hi, lo = split2(block)
            in_col = in_col_ref[b]
            at_col = dot(jnp.concatenate([hi, lo], axis=1), jnp.concatenate([in_col, in_col], axis=0))
            band_ref[m, i : i + 1, :] = jnp.sum(
                at_col * in_row_ref[b].astype(F32), axis=0, keepdims=True
            )


def late_kernel(*refs):
    xs, ds, wgu_ref, wd_ref, own_ref, got_ref = refs[:2], refs[2:4], *refs[4:8]
    side = own_ref.shape[1]
    x = jnp.concatenate([ref[...] for ref in xs], axis=0)
    d = jnp.concatenate([ref[...] for ref in ds], axis=0)
    wgu = jnp.concatenate([wgu_ref[:side, :], wgu_ref[2 * side : 3 * side, :]], axis=0)
    d_gate, d_up, hidden = activations(wgu, wd_ref[:side, :], x, d)
    late = (dot(d_gate, x), dot(d_up, x), dot(hidden, d))
    grads = [late[m] + (own_ref[m] + got_ref[m]) for m in range(3)]
    moment_step(grads, refs[8:11], *refs[11:])


def moment_kernel(grad_ref, *refs):
    moment_step([grad_ref[m] for m in range(3)], refs[:3], *refs[3:])


def residual_kernel(moment_ref, coeffs_ref, in_row_ref, in_col_t_ref, cosines_ref, cosines_t_ref, *outs):
    *residuals, decoded_ref, cells_ref = outs
    side = cosines_ref.shape[0]
    count = residuals[0].shape[0]
    blocks = range(3 * count)
    cosines = cosines_ref[...]
    band = [coeffs_ref[b] * dot(in_row_ref[b], in_col_t_ref[b]) for b in blocks]
    inner = dot3(jnp.concatenate(band, axis=0), cosines)
    inner = jnp.concatenate([inner[b * side : (b + 1) * side] for b in blocks], axis=1)
    decoded = dot3(cosines_t_ref[...], inner)
    for b in blocks:
        kept = decoded[:, b * side : (b + 1) * side]
        decoded_ref[b] = kept
        residuals[b // count][b % count] = moment_ref[b] - kept
    parts = jnp.concatenate(split2(cosines), axis=1)
    for b in blocks:
        cells_ref[b] = dot(in_col_t_ref[b], parts).astype(BF16)


def update_kernel(decoded_ref, other_ref, in_row_ref, cells_ref, cosines_t_ref, *outs):
    side = cosines_t_ref.shape[0]
    count = outs[0].shape[0]
    inner = []
    for b in range(3 * count):
        m, i = b // count, b % count
        hi, lo = split2(sum(other_ref[g, m, i : i + 1, :] for g in range(other_ref.shape[0])))
        in_row = in_row_ref[b]
        both = dot(jnp.concatenate([in_row * hi, in_row * lo], axis=0), cells_ref[b])
        inner.append(both[:side, :side] + (both[:side, side:] + both[side:, :side]))
    update = dot3(cosines_t_ref[...], jnp.concatenate(inner, axis=1))
    for b in range(3 * count):
        outs[b // count][b % count] = decoded_ref[b] + update[:, b * side : (b + 1) * side]


def call(kernel, out_shape, flops, *args, scratch=(), in_place={}):
    moved = sum(a.size * a.dtype.itemsize for a in args)
    specs = [
        pl.BlockSpec(memory_space=in_place.get(k, pltpu.VMEM)) for k in range(len(args))
    ]
    return pl.pallas_call(
        kernel,
        out_shape=out_shape,
        in_specs=specs,
        scratch_shapes=list(scratch),
        compiler_params=pltpu.CompilerParams(vmem_limit_bytes=24 * 1024 * 1024),
        cost_estimate=pl.CostEstimate(flops=flops, bytes_accessed=2 * moved, transcendentals=0),
    )(*args)


def ring_perms(count):
    chips = count // 2
    order = list(range(0, chips, 2)) + list(range(1, chips, 2))[::-1]
    forward = [
        (2 * order[p] + c, 2 * order[(p + 1) % chips] + c) for p in range(chips) for c in range(2)
    ]
    return forward, [(b, a) for a, b in forward], chips


def after(kernel, out_shape, flops, band_index, *ahead):
    in_place = dict.fromkeys(range(1, 1 + len(ahead)), pl.ANY)
    return call(kernel, out_shape, flops, band_index, *ahead, in_place=in_place)


def band_tables(band_index, side, *ahead):
    blocks, keep = band_index.shape[0] * band_index.shape[1], band_index.shape[2]
    hots = jax.ShapeDtypeStruct((blocks, side, keep), BF16)
    return after(tables_kernel, (hots, hots), TABLES_FLOPS, band_index, *ahead)


def band_columns(band_index, side, *ahead):
    blocks, keep = band_index.shape[0] * band_index.shape[1], band_index.shape[2]
    hots = jax.ShapeDtypeStruct((blocks, keep, side), BF16)
    return after(columns_kernel, hots, COLUMNS_FLOPS, band_index, *ahead)


def column_moments(x, d, weights, momenta, band_index, cosines, cosines_t, shapes):
    side = weights[0].shape[1]
    rows, width = x.shape
    count = lax.axis_size("fsdp")
    swap = [(f, f ^ 1) for f in range(count)]
    forward, back, chips = ring_perms(count)

    def send(value, perm):
        return lax.ppermute(value, "fsdp", perm)

    xf, db, df, xb = send(x, forward), send(d, back), send(d, forward), send(x, back)
    xs, ds = [x, xf, xb], [d, df, db]
    partner_weights = [send(w, swap) for w in weights]
    pause = call(pause_kernel, jax.ShapeDtypeStruct((8, 128), F32), PAUSE_FLOPS)
    db, pause = lax.optimization_barrier((db, pause))
    arrived = []

    def with_weight(value):
        if len(arrived) == len(partner_weights):
            return value
        value, weight = lax.optimization_barrier((value, partner_weights[len(arrived)]))
        arrived.append(weight)
        return value

    for _ in range(chips // 2 - 2):
        db = with_weight(db)
        xf, db, df, xb = send(xf, forward), send(db, back), send(df, forward), send(xb, back)
        xs += [xf, xb]
        ds += [df, db]
    x_last, d_last = send(xf, forward), send(with_weight(db), back)
    partner_weights[: len(arrived)] = arrived

    def scratch(shards):
        return (
            pltpu.VMEM((shards * rows, width), BF16),
            pltpu.VMEM((shards * rows, width), BF16),
            pltpu.VMEM((6 * side, shards * rows), BF16),
        )

    part = jax.ShapeDtypeStruct((3, side, width), F32)
    early = len(xs) - 2
    own, partner, wgu, wd = call(
        functools.partial(early_kernel, early),
        (
            part,
            part,
            jax.ShapeDtypeStruct((4 * side, width), BF16),
            jax.ShapeDtypeStruct((2 * side, width), BF16),
        ),
        24 * early * rows * width * side,
        *xs[:early],
        *ds[:early],
        *weights,
        *partner_weights,
        pause,
        scratch=scratch(early),
    )
    own, partner = call(
        functools.partial(middle_kernel, 2),
        (part, part),
        24 * 2 * rows * width * side,
        *xs[early:],
        *ds[early:],
        wgu,
        wd,
        own,
        partner,
        scratch=scratch(2),
    )
    got = send(partner, swap)
    x_swap, d_swap = send(x_last, swap), send(d_last, swap)
    in_col_t = band_columns(band_index, side, partner)
    in_row, in_col = band_tables(band_index, side, x_last, d_last)
    moments = call(
        late_kernel,
        shapes,
        10**9,
        x_last,
        x_swap,
        d_last,
        d_swap,
        wgu,
        wd,
        own,
        got,
        *momenta,
        in_row,
        in_col,
        cosines,
        cosines_t,
    )
    return moments, in_row, in_col_t


def shared_column_moments(x, d, weights, momenta, band_index, cosines, cosines_t, shapes):
    gate_weight, up_weight, down_weight = weights
    own = shared_column_grads(x, d, gate_weight, up_weight, down_weight)
    in_col_t = band_columns(band_index, cosines.shape[0], own)
    in_row, in_col = band_tables(band_index, cosines.shape[0], own)
    moments = call(
        moment_kernel,
        shapes,
        0,
        own,
        *momenta,
        in_row,
        in_col,
        cosines,
        cosines_t,
    )
    return moments, in_row, in_col_t


def shared_column_grads(x, d, gate_weight, up_weight, down_weight):
    side = gate_weight.shape[1]
    width = x.shape[1]
    blk_dev = gate_weight.shape[0]
    count = lax.axis_size("fsdp")
    share = width // side // blk_dev
    groups = [list(range(g * share, (g + 1) * share)) for g in range(count // share)]

    def whole(w):
        return lax.all_gather(w, "fsdp", axis=0, tiled=True, axis_index_groups=groups)

    gate, up = whole(gate_weight).reshape(width, side), whole(up_weight).reshape(width, side)
    down = whole(down_weight).transpose(1, 0, 2).reshape(side, width)
    x_all = lax.all_gather(x, "fsdp", axis=0, tiled=True)
    d_all = lax.all_gather(d, "fsdp", axis=0, tiled=True)
    gate_pre = jnp.dot(x_all, gate, preferred_element_type=F32)
    up_pre = jnp.dot(x_all, up, preferred_element_type=F32)
    d_hidden = jnp.dot(d_all, down.T, preferred_element_type=F32)
    sig = jax.nn.sigmoid(gate_pre)
    hidden = (gate_pre * sig * up_pre).astype(BF16)
    d_gate = (d_hidden * up_pre * sig * (1.0 + gate_pre * (1.0 - sig))).astype(BF16)
    d_up = (d_hidden * gate_pre * sig).astype(BF16)
    start = lax.rem(lax.axis_index("fsdp"), share) * blk_dev * side
    x_own = lax.dynamic_slice_in_dim(x_all, start, blk_dev * side, axis=1)
    d_own = lax.dynamic_slice_in_dim(d_all, start, blk_dev * side, axis=1)
    own = jnp.stack(
        [
            jnp.dot(d_gate.T, x_own, preferred_element_type=F32),
            jnp.dot(d_up.T, x_own, preferred_element_type=F32),
            jnp.dot(hidden.T, d_own, preferred_element_type=F32),
        ]
    )
    return own


def per_device(
    x_in, d_out, gate_weight, up_weight, down_weight, mom_gate, mom_up, mom_down, band_index
):
    side = gate_weight.shape[1]
    blk_dev = gate_weight.shape[0]
    row_blocks = x_in.shape[2] // side
    if blk_dev == row_blocks and lax.axis_size("fsdp") % 4 == 0:
        step = column_moments
    else:
        step = shared_column_moments
    cosines, cosines_t = jnp.asarray(dct_table(side)), jnp.asarray(dct_table(side).T)
    blocks = 3 * blk_dev
    dense = jax.ShapeDtypeStruct((blocks, side, side), F32)
    (moment, coeffs, band), in_row, in_col_t = step(
        x_in[0],
        d_out[0],
        (gate_weight, up_weight, down_weight),
        (mom_gate[0], mom_up[0], mom_down[0]),
        band_index,
        cosines,
        cosines_t,
        (dense, dense, jax.ShapeDtypeStruct(band_index.shape, F32)),
    )
    reps = lax.axis_size("rep")
    other = jnp.stack(
        [
            lax.ppermute(band, "rep", [(r, (r + s) % reps) for r in range(reps)])
            for s in range(1, reps)
        ]
    )
    result = jax.ShapeDtypeStruct((blk_dev, side, side), F32)
    flops = 4 * 3 * blocks * side**3
    *residuals, decoded, cells = call(
        residual_kernel,
        (result,) * 3 + (dense, jax.ShapeDtypeStruct((*in_col_t.shape[:2], 2 * side), BF16)),
        flops,
        moment,
        coeffs,
        in_row,
        in_col_t,
        cosines,
        cosines_t,
    )
    updates = call(
        update_kernel, (result,) * 3, flops, decoded, other, in_row, cells, cosines_t
    )
    return (*(r[None] for r in residuals), *updates)


def solution(mesh):
    in_specs = (
        P("rep", "fsdp", None),
        P("rep", "fsdp", None),
        P("fsdp", None, None),
        P("fsdp", None, None),
        P("fsdp", None, None),
        P("rep", "fsdp", None, None),
        P("rep", "fsdp", None, None),
        P("rep", "fsdp", None, None),
        P(None, "fsdp", None),
    )
    out_specs = (
        P("rep", "fsdp", None, None),
        P("rep", "fsdp", None, None),
        P("rep", "fsdp", None, None),
        P("fsdp", None, None),
        P("fsdp", None, None),
        P("fsdp", None, None),
    )
    return jax.shard_map(
        per_device, mesh=mesh, in_specs=in_specs, out_specs=out_specs, check_vma=False
    )
```

```python
import functools

import jax
import jax.numpy as jnp
import numpy as np
from jax import lax
from jax.experimental import pallas as pl
from jax.experimental.pallas import tpu as pltpu
from jax.sharding import PartitionSpec as P

MOMENTUM_DECAY = 0.999
TABLES_FLOPS = 10**10
COLUMNS_FLOPS = 10**9
PAUSE_FLOPS = 10**9
F32 = jnp.float32
BF16 = jnp.bfloat16


def dct_table(side):
    k = np.arange(side, dtype=np.float64)[:, None]
    n = np.arange(side, dtype=np.float64)[None, :]
    scale = np.where(k == 0, np.sqrt(1.0 / side), np.sqrt(2.0 / side))
    return (scale * np.cos(np.pi * (2.0 * n + 1.0) * k / (2.0 * side))).astype(np.float32)


def split2(value):
    hi = value.astype(BF16)
    return hi, (value - hi.astype(F32)).astype(BF16)


def dot(a, b):
    return jnp.dot(a, b, preferred_element_type=F32)


def dot_nt(a, b):
    return lax.dot_general(a, b, (((1,), (1,)), ((), ())), preferred_element_type=F32)


def dot3(a, b):
    a_hi, a_lo = split2(a)
    b_hi, b_lo = split2(b)
    left = jnp.concatenate([a_hi, a_hi, a_lo], axis=1)
    return dot(left, jnp.concatenate([b_hi, b_lo, b_hi], axis=0))


def lanes_to_rows(value, side):
    count = value.shape[1] // side
    return jnp.concatenate([value[:, i * side : (i + 1) * side] for i in range(count)], axis=0)


def activations(wgu, wd, x, d):
    pre = dot_nt(wgu, x)
    dh = dot_nt(wd, d)
    gate, up = pre[: wd.shape[0]], pre[wd.shape[0] :]
    sig = jax.nn.sigmoid(gate)
    swish = gate * sig
    d_gate = (dh * up * sig * (1.0 + gate * (1.0 - sig))).astype(BF16)
    return d_gate, (dh * swish).astype(BF16), (swish * up).astype(BF16)


def one_hot(numbers, lines):
    return jnp.where(numbers == lines, 1.0, 0.0).astype(BF16)


def tables_kernel(index_ref, *refs):
    in_row_ref, in_col_ref = refs[-2:]
    blocks, side, keep = in_row_ref.shape
    count = index_ref.shape[1]
    shift = int(np.log2(side))
    lines = lax.broadcasted_iota(jnp.int32, (side, keep), 0)
    for b in range(blocks):
        index = index_ref[b // count, b % count : b % count + 1, :]
        in_row_ref[b] = one_hot(index >> shift, lines)
        in_col_ref[b] = one_hot(index & (side - 1), lines)


def columns_kernel(index_ref, *refs):
    out_ref = refs[-1]
    blocks, keep, side = out_ref.shape
    count = index_ref.shape[1]
    lines = lax.broadcasted_iota(jnp.int32, (side, keep), 0)
    for b in range(blocks):
        index = index_ref[b // count, b % count : b % count + 1, :]
        out_ref[b] = one_hot(index & (side - 1), lines).T


def pause_kernel(out_ref):
    out_ref[...] = jnp.zeros_like(out_ref)


def column_grads(xs, ds, wgu, wd, x_all, d_all, act):
    rows, half = xs[0].shape[0], wd.shape[0]
    for s in range(0, len(xs), 2):
        some = range(s, min(s + 2, len(xs)))
        x = jnp.concatenate([xs[j][...] for j in some], axis=0)
        d = jnp.concatenate([ds[j][...] for j in some], axis=0)
        span = pl.ds(s * rows, len(some) * rows)
        x_all[span, :] = x
        d_all[span, :] = d
        d_gate, d_up, hidden = activations(wgu, wd, x, d)
        act[:half, span] = d_gate
        act[half : 2 * half, span] = d_up
        act[2 * half :, span] = hidden
    g_in = dot(act[: 2 * half, :], x_all[...])
    return g_in[:half], g_in[half:], dot(act[2 * half :, :], d_all[...])


def early_kernel(shards, *refs):
    xs, ds, weights = refs[:shards], refs[shards : 2 * shards], refs[2 * shards : 2 * shards + 6]
    own_ref, par_ref, wgu_ref, wd_ref, *scratch = refs[2 * shards + 7 :]
    count, side, _ = weights[0].shape
    for i in range(count):
        cols = slice(i * side, (i + 1) * side)
        for p in range(2):
            gate, up, down = (ref[i] for ref in weights[3 * p : 3 * p + 3])
            wgu_ref[p * side : (p + 1) * side, cols] = gate.T
            wgu_ref[(2 + p) * side : (3 + p) * side, cols] = up.T
            wd_ref[p * side : (p + 1) * side, cols] = down
    for m, grad in enumerate(column_grads(xs, ds, wgu_ref[...], wd_ref[...], *scratch)):
        own_ref[m] = grad[:side]
        par_ref[m] = grad[side:]


def middle_kernel(shards, *refs):
    xs, ds = refs[:shards], refs[shards : 2 * shards]
    wgu_ref, wd_ref, own_in, par_in, own_ref, par_ref, *scratch = refs[2 * shards :]
    side = own_ref.shape[1]
    count = own_ref.shape[0] // 3
    for m, grad in enumerate(column_grads(xs, ds, wgu_ref[...], wd_ref[...], *scratch)):
        for add_ref, out_ref, part in (
            (own_in, own_ref, grad[:side]),
            (par_in, par_ref, grad[side:]),
        ):
            total = add_ref[m] + part
            for i in range(count):
                piece = total[:, i * side : (i + 1) * side]
                out_ref[m * count + i] = piece.T if m < 2 else piece


def moment_step(
    grads, mom_refs, in_row_ref, in_col_ref, cosines_ref, cosines_t_ref, moment_ref, coeffs_ref, band_ref
):
    side = cosines_ref.shape[0]
    count = mom_refs[0].shape[0]
    blocks = []
    for b, grad in enumerate(grads):
        block = MOMENTUM_DECAY * mom_refs[b // count][b % count] + grad
        moment_ref[b] = block
        blocks.append(block)
    inner = dot3(cosines_ref[...], jnp.concatenate(blocks, axis=1))
    coeffs = dot3(lanes_to_rows(inner, side), cosines_t_ref[...])
    for m in range(3):
        for i in range(count):
            b = m * count + i
            block = coeffs[b * side : (b + 1) * side]
            coeffs_ref[b] = block
            hi, lo = split2(block)
            in_col = in_col_ref[b]
            at_col = dot(jnp.concatenate([hi, lo], axis=1), jnp.concatenate([in_col, in_col], axis=0))
            band_ref[m, i : i + 1, :] = jnp.sum(
                at_col * in_row_ref[b].astype(F32), axis=0, keepdims=True
            )


def late_kernel(*refs):
    xs, ds, wgu_ref, wd_ref, own_ref, got_ref = refs[:2], refs[2:4], *refs[4:8]
    side = own_ref.shape[1]
    count = own_ref.shape[0] // 3
    x = jnp.concatenate([ref[...] for ref in xs], axis=0)
    d = jnp.concatenate([ref[...] for ref in ds], axis=0)
    x_t = x.T
    wgu = jnp.concatenate([wgu_ref[:side, :], wgu_ref[2 * side : 3 * side, :]], axis=0)
    d_gate, d_up, hidden = activations(wgu, wd_ref[:side, :], x, d)
    g_in = dot_nt(x_t, jnp.concatenate([d_gate, d_up], axis=0))
    g_out = dot(hidden, d)
    late = [
        g_in[i * side : (i + 1) * side, m * side : (m + 1) * side]
        for m in range(2)
        for i in range(count)
    ]
    late += [g_out[:, i * side : (i + 1) * side] for i in range(count)]
    grads = [late[b] + (own_ref[b] + got_ref[b]) for b in range(3 * count)]
    moment_step(grads, refs[8:11], *refs[11:])


def moment_kernel(grad_ref, *refs):
    moment_step([grad_ref[b] for b in range(grad_ref.shape[0])], refs[:3], *refs[3:])


def residual_kernel(moment_ref, coeffs_ref, in_row_ref, in_col_t_ref, cosines_ref, cosines_t_ref, *outs):
    *residuals, decoded_ref, cells_ref = outs
    side = cosines_ref.shape[0]
    count = residuals[0].shape[0]
    blocks = range(3 * count)
    cosines = cosines_ref[...]
    band = [coeffs_ref[b] * dot(in_row_ref[b], in_col_t_ref[b]) for b in blocks]
    inner = dot3(jnp.concatenate(band, axis=0), cosines)
    inner = jnp.concatenate([inner[b * side : (b + 1) * side] for b in blocks], axis=1)
    decoded = dot3(cosines_t_ref[...], inner)
    for b in blocks:
        kept = decoded[:, b * side : (b + 1) * side]
        decoded_ref[b] = kept
        residuals[b // count][b % count] = moment_ref[b] - kept
    parts = jnp.concatenate(split2(cosines), axis=1)
    for b in blocks:
        cells_ref[b] = dot(in_col_t_ref[b], parts).astype(BF16)


def update_kernel(decoded_ref, other_ref, in_row_ref, cells_ref, cosines_t_ref, *outs):
    side = cosines_t_ref.shape[0]
    count = outs[0].shape[0]
    inner = []
    for b in range(3 * count):
        m, i = b // count, b % count
        hi, lo = split2(sum(other_ref[g, m, i : i + 1, :] for g in range(other_ref.shape[0])))
        in_row = in_row_ref[b]
        both = dot(jnp.concatenate([in_row * hi, in_row * lo], axis=0), cells_ref[b])
        inner.append(both[:side, :side] + (both[:side, side:] + both[side:, :side]))
    update = dot3(cosines_t_ref[...], jnp.concatenate(inner, axis=1))
    for b in range(3 * count):
        outs[b // count][b % count] = decoded_ref[b] + update[:, b * side : (b + 1) * side]


def call(kernel, out_shape, flops, *args, scratch=(), in_place={}):
    moved = sum(a.size * a.dtype.itemsize for a in args)
    specs = [
        pl.BlockSpec(memory_space=in_place.get(k, pltpu.VMEM)) for k in range(len(args))
    ]
    return pl.pallas_call(
        kernel,
        out_shape=out_shape,
        in_specs=specs,
        scratch_shapes=list(scratch),
        compiler_params=pltpu.CompilerParams(vmem_limit_bytes=24 * 1024 * 1024),
        cost_estimate=pl.CostEstimate(flops=flops, bytes_accessed=2 * moved, transcendentals=0),
    )(*args)


def ring_perms(count):
    chips = count // 2
    order = list(range(0, chips, 2)) + list(range(1, chips, 2))[::-1]
    forward = [
        (2 * order[p] + c, 2 * order[(p + 1) % chips] + c) for p in range(chips) for c in range(2)
    ]
    return forward, [(b, a) for a, b in forward], chips


def after(kernel, out_shape, flops, band_index, *ahead):
    in_place = dict.fromkeys(range(1, 1 + len(ahead)), pl.ANY)
    return call(kernel, out_shape, flops, band_index, *ahead, in_place=in_place)


def band_tables(band_index, side, *ahead):
    blocks, keep = band_index.shape[0] * band_index.shape[1], band_index.shape[2]
    hots = jax.ShapeDtypeStruct((blocks, side, keep), BF16)
    return after(tables_kernel, (hots, hots), TABLES_FLOPS, band_index, *ahead)


def band_columns(band_index, side, *ahead):
    blocks, keep = band_index.shape[0] * band_index.shape[1], band_index.shape[2]
    hots = jax.ShapeDtypeStruct((blocks, keep, side), BF16)
    return after(columns_kernel, hots, COLUMNS_FLOPS, band_index, *ahead)


def column_moments(x, d, weights, momenta, band_index, cosines, cosines_t, shapes):
    side = weights[0].shape[1]
    rows, width = x.shape
    count = lax.axis_size("fsdp")
    swap = [(f, f ^ 1) for f in range(count)]
    forward, back, chips = ring_perms(count)

    def send(value, perm):
        return lax.ppermute(value, "fsdp", perm)

    xf, db, df, xb = send(x, forward), send(d, back), send(d, forward), send(x, back)
    xs, ds = [x, xf, xb], [d, df, db]
    partner_weights = [send(w, swap) for w in weights]
    pause = call(pause_kernel, jax.ShapeDtypeStruct((8, 128), F32), PAUSE_FLOPS)
    db, pause = lax.optimization_barrier((db, pause))
    arrived = []

    def with_weight(value):
        if len(arrived) == len(partner_weights):
            return value
        value, weight = lax.optimization_barrier((value, partner_weights[len(arrived)]))
        arrived.append(weight)
        return value

    for _ in range(chips // 2 - 2):
        db = with_weight(db)
        xf, db, df, xb = send(xf, forward), send(db, back), send(df, forward), send(xb, back)
        xs += [xf, xb]
        ds += [df, db]
    x_last, d_last = send(xf, forward), send(with_weight(db), back)
    partner_weights[: len(arrived)] = arrived

    def scratch(shards):
        return (
            pltpu.VMEM((shards * rows, width), BF16),
            pltpu.VMEM((shards * rows, width), BF16),
            pltpu.VMEM((6 * side, shards * rows), BF16),
        )

    part = jax.ShapeDtypeStruct((3, side, width), F32)
    early = len(xs) - 2
    own, partner, wgu, wd = call(
        functools.partial(early_kernel, early),
        (
            part,
            part,
            jax.ShapeDtypeStruct((4 * side, width), BF16),
            jax.ShapeDtypeStruct((2 * side, width), BF16),
        ),
        24 * early * rows * width * side,
        *xs[:early],
        *ds[:early],
        *weights,
        *partner_weights,
        pause,
        scratch=scratch(early),
    )
    own, partner = call(
        functools.partial(middle_kernel, 2),
        (shapes[0], shapes[0]),
        24 * 2 * rows * width * side,
        *xs[early:],
        *ds[early:],
        wgu,
        wd,
        own,
        partner,
        scratch=scratch(2),
    )
    got = send(partner, swap)
    x_swap, d_swap = send(x_last, swap), send(d_last, swap)
    in_col_t = band_columns(band_index, side, partner)
    in_row, in_col = band_tables(band_index, side, x_last, d_last)
    moments = call(
        late_kernel,
        shapes,
        10**9,
        x_last,
        x_swap,
        d_last,
        d_swap,
        wgu,
        wd,
        own,
        got,
        *momenta,
        in_row,
        in_col,
        cosines,
        cosines_t,
    )
    return moments, in_row, in_col_t


def shared_column_moments(x, d, weights, momenta, band_index, cosines, cosines_t, shapes):
    gate_weight, up_weight, down_weight = weights
    own = shared_column_grads(x, d, gate_weight, up_weight, down_weight)
    side = cosines.shape[0]
    cut = own.reshape(3, side, -1, side)
    own = jnp.concatenate([cut[:2].transpose(0, 2, 3, 1), cut[2:].transpose(0, 2, 1, 3)], axis=0)
    own = own.reshape(-1, side, side)
    in_col_t = band_columns(band_index, cosines.shape[0], own)
    in_row, in_col = band_tables(band_index, cosines.shape[0], own)
    moments = call(
        moment_kernel,
        shapes,
        0,
        own,
        *momenta,
        in_row,
        in_col,
        cosines,
        cosines_t,
    )
    return moments, in_row, in_col_t


def shared_column_grads(x, d, gate_weight, up_weight, down_weight):
    side = gate_weight.shape[1]
    width = x.shape[1]
    blk_dev = gate_weight.shape[0]
    count = lax.axis_size("fsdp")
    share = width // side // blk_dev
    groups = [list(range(g * share, (g + 1) * share)) for g in range(count // share)]

    def whole(w):
        return lax.all_gather(w, "fsdp", axis=0, tiled=True, axis_index_groups=groups)

    gate, up = whole(gate_weight).reshape(width, side), whole(up_weight).reshape(width, side)
    down = whole(down_weight).transpose(1, 0, 2).reshape(side, width)
    x_all = lax.all_gather(x, "fsdp", axis=0, tiled=True)
    d_all = lax.all_gather(d, "fsdp", axis=0, tiled=True)
    gate_pre = jnp.dot(x_all, gate, preferred_element_type=F32)
    up_pre = jnp.dot(x_all, up, preferred_element_type=F32)
    d_hidden = jnp.dot(d_all, down.T, preferred_element_type=F32)
    sig = jax.nn.sigmoid(gate_pre)
    hidden = (gate_pre * sig * up_pre).astype(BF16)
    d_gate = (d_hidden * up_pre * sig * (1.0 + gate_pre * (1.0 - sig))).astype(BF16)
    d_up = (d_hidden * gate_pre * sig).astype(BF16)
    start = lax.rem(lax.axis_index("fsdp"), share) * blk_dev * side
    x_own = lax.dynamic_slice_in_dim(x_all, start, blk_dev * side, axis=1)
    d_own = lax.dynamic_slice_in_dim(d_all, start, blk_dev * side, axis=1)
    own = jnp.stack(
        [
            jnp.dot(d_gate.T, x_own, preferred_element_type=F32),
            jnp.dot(d_up.T, x_own, preferred_element_type=F32),
            jnp.dot(hidden.T, d_own, preferred_element_type=F32),
        ]
    )
    return own


def per_device(
    x_in, d_out, gate_weight, up_weight, down_weight, mom_gate, mom_up, mom_down, band_index
):
    side = gate_weight.shape[1]
    blk_dev = gate_weight.shape[0]
    row_blocks = x_in.shape[2] // side
    if blk_dev == row_blocks and lax.axis_size("fsdp") % 4 == 0:
        step = column_moments
    else:
        step = shared_column_moments
    cosines, cosines_t = jnp.asarray(dct_table(side)), jnp.asarray(dct_table(side).T)
    blocks = 3 * blk_dev
    dense = jax.ShapeDtypeStruct((blocks, side, side), F32)
    (moment, coeffs, band), in_row, in_col_t = step(
        x_in[0],
        d_out[0],
        (gate_weight, up_weight, down_weight),
        (mom_gate[0], mom_up[0], mom_down[0]),
        band_index,
        cosines,
        cosines_t,
        (dense, dense, jax.ShapeDtypeStruct(band_index.shape, F32)),
    )
    reps = lax.axis_size("rep")
    other = jnp.stack(
        [
            lax.ppermute(band, "rep", [(r, (r + s) % reps) for r in range(reps)])
            for s in range(1, reps)
        ]
    )
    result = jax.ShapeDtypeStruct((blk_dev, side, side), F32)
    flops = 4 * 3 * blocks * side**3
    *residuals, decoded, cells = call(
        residual_kernel,
        (result,) * 3 + (dense, jax.ShapeDtypeStruct((*in_col_t.shape[:2], 2 * side), BF16)),
        flops,
        moment,
        coeffs,
        in_row,
        in_col_t,
        cosines,
        cosines_t,
    )
    updates = call(
        update_kernel, (result,) * 3, flops, decoded, other, in_row, cells, cosines_t
    )
    return (*(r[None] for r in residuals), *updates)


def solution(mesh):
    in_specs = (
        P("rep", "fsdp", None),
        P("rep", "fsdp", None),
        P("fsdp", None, None),
        P("fsdp", None, None),
        P("fsdp", None, None),
        P("rep", "fsdp", None, None),
        P("rep", "fsdp", None, None),
        P("rep", "fsdp", None, None),
        P(None, "fsdp", None),
    )
    out_specs = (
        P("rep", "fsdp", None, None),
        P("rep", "fsdp", None, None),
        P("rep", "fsdp", None, None),
        P("fsdp", None, None),
        P("fsdp", None, None),
        P("fsdp", None, None),
    )
    return jax.shard_map(
        per_device, mesh=mesh, in_specs=in_specs, out_specs=out_specs, check_vma=False
    )
```

```python
import functools

import jax
import jax.numpy as jnp
import numpy as np
from jax import lax
from jax.experimental import pallas as pl
from jax.experimental.pallas import tpu as pltpu
from jax.sharding import PartitionSpec as P

MOMENTUM_DECAY = 0.999
TABLES_FLOPS = 10**10
COLUMNS_FLOPS = 10**9
PAUSE_FLOPS = 10**9
F32 = jnp.float32
BF16 = jnp.bfloat16


def dct_table(side):
    k = np.arange(side, dtype=np.float64)[:, None]
    n = np.arange(side, dtype=np.float64)[None, :]
    scale = np.where(k == 0, np.sqrt(1.0 / side), np.sqrt(2.0 / side))
    return (scale * np.cos(np.pi * (2.0 * n + 1.0) * k / (2.0 * side))).astype(np.float32)


def split2(value):
    hi = value.astype(BF16)
    return hi, (value - hi.astype(F32)).astype(BF16)


def dot(a, b):
    return jnp.dot(a, b, preferred_element_type=F32)


def dot_nt(a, b):
    return lax.dot_general(a, b, (((1,), (1,)), ((), ())), preferred_element_type=F32)


def dot3(a, b):
    a_hi, a_lo = split2(a)
    b_hi, b_lo = split2(b)
    left = jnp.concatenate([a_hi, a_hi, a_lo], axis=1)
    return dot(left, jnp.concatenate([b_hi, b_lo, b_hi], axis=0))


def lanes_to_rows(value, side):
    count = value.shape[1] // side
    return jnp.concatenate([value[:, i * side : (i + 1) * side] for i in range(count)], axis=0)


def activations(wgu, wd, x, d):
    pre = dot_nt(wgu, x)
    dh = dot_nt(wd, d)
    gate, up = pre[: wd.shape[0]], pre[wd.shape[0] :]
    sig = jax.nn.sigmoid(gate)
    swish = gate * sig
    d_gate = (dh * up * sig * (1.0 + gate * (1.0 - sig))).astype(BF16)
    return d_gate, (dh * swish).astype(BF16), (swish * up).astype(BF16)


def one_hot(numbers, lines):
    return jnp.where(numbers == lines, 1.0, 0.0).astype(BF16)


def tables_kernel(index_ref, *refs):
    in_row_ref, in_col_ref = refs[-2:]
    blocks, side, keep = in_row_ref.shape
    count = index_ref.shape[1]
    shift = int(np.log2(side))
    lines = lax.broadcasted_iota(jnp.int32, (side, keep), 0)
    for b in range(blocks):
        index = index_ref[b // count, b % count : b % count + 1, :]
        in_row_ref[b] = one_hot(index >> shift, lines)
        in_col_ref[b] = one_hot(index & (side - 1), lines)


def columns_kernel(index_ref, *refs):
    out_ref = refs[-1]
    blocks, keep, side = out_ref.shape
    count = index_ref.shape[1]
    lines = lax.broadcasted_iota(jnp.int32, (side, keep), 0)
    for b in range(blocks):
        index = index_ref[b // count, b % count : b % count + 1, :]
        out_ref[b] = one_hot(index & (side - 1), lines).T


def pause_kernel(out_ref):
    out_ref[...] = jnp.zeros_like(out_ref)


def column_grads(xs, ds, wgu, wd, x_all, d_all, act):
    rows, half = xs[0].shape[0], wd.shape[0]
    for s in range(0, len(xs), 2):
        some = range(s, min(s + 2, len(xs)))
        x = jnp.concatenate([xs[j][...] for j in some], axis=0)
        d = jnp.concatenate([ds[j][...] for j in some], axis=0)
        span = pl.ds(s * rows, len(some) * rows)
        x_all[span, :] = x
        d_all[span, :] = d
        d_gate, d_up, hidden = activations(wgu, wd, x, d)
        act[:half, span] = d_gate
        act[half : 2 * half, span] = d_up
        act[2 * half :, span] = hidden
    g_in = dot(act[: 2 * half, :], x_all[...])
    return g_in[:half], g_in[half:], dot(act[2 * half :, :], d_all[...])


def early_kernel(shards, *refs):
    xs, ds, weights = refs[:shards], refs[shards : 2 * shards], refs[2 * shards : 2 * shards + 6]
    own_ref, par_ref, wgu_ref, wd_ref, *scratch = refs[2 * shards + 7 :]
    count, side, _ = weights[0].shape
    for i in range(count):
        cols = slice(i * side, (i + 1) * side)
        for p in range(2):
            gate, up, down = (ref[i] for ref in weights[3 * p : 3 * p + 3])
            wgu_ref[p * side : (p + 1) * side, cols] = gate.T
            wgu_ref[(2 + p) * side : (3 + p) * side, cols] = up.T
            wd_ref[p * side : (p + 1) * side, cols] = down
    for m, grad in enumerate(column_grads(xs, ds, wgu_ref[...], wd_ref[...], *scratch)):
        own_ref[m] = grad[:side]
        par_ref[m] = grad[side:]


def middle_kernel(shards, *refs):
    xs, ds = refs[:shards], refs[shards : 2 * shards]
    wgu_ref, wd_ref, own_in, par_in, own_ref, par_ref, *scratch = refs[2 * shards :]
    side = own_ref.shape[1]
    for m, grad in enumerate(column_grads(xs, ds, wgu_ref[...], wd_ref[...], *scratch)):
        own_ref[m] = own_in[m] + grad[:side]
        par_ref[m] = par_in[m] + grad[side:]


def moment_step(
    grads, mom_refs, in_row_ref, in_col_ref, cosines_ref, cosines_t_ref, moment_ref, coeffs_ref, band_ref
):
    side = cosines_ref.shape[0]
    count = mom_refs[0].shape[0]
    blocks = []
    for m in range(3):
        for i in range(count):
            piece = grads[m][:, i * side : (i + 1) * side]
            if m < 2:
                piece = piece.T
            block = MOMENTUM_DECAY * mom_refs[m][i] + piece
            moment_ref[m * count + i] = block
            blocks.append(block)
    inner = dot3(cosines_ref[...], jnp.concatenate(blocks, axis=1))
    coeffs = dot3(lanes_to_rows(inner, side), cosines_t_ref[...])
    for m in range(3):
        for i in range(count):
            b = m * count + i
            block = coeffs[b * side : (b + 1) * side]
            coeffs_ref[b] = block
            hi, lo = split2(block)
            in_col = in_col_ref[b]
            at_col = dot(jnp.concatenate([hi, lo], axis=1), jnp.concatenate([in_col, in_col], axis=0))
            band_ref[m, i : i + 1, :] = jnp.sum(
                at_col * in_row_ref[b].astype(F32), axis=0, keepdims=True
            )


def late_kernel(*refs):
    xs, ds, wgu_ref, wd_ref, own_ref, got_ref = refs[:2], refs[2:4], *refs[4:8]
    side = own_ref.shape[1]
    x = jnp.concatenate([ref[...] for ref in xs], axis=0)
    d = jnp.concatenate([ref[...] for ref in ds], axis=0)
    wgu = jnp.concatenate([wgu_ref[:side, :], wgu_ref[2 * side : 3 * side, :]], axis=0)
    d_gate, d_up, hidden = activations(wgu, wd_ref[:side, :], x, d)
    late = (dot(d_gate, x), dot(d_up, x), dot(hidden, d))
    grads = [late[m] + (own_ref[m] + got_ref[m]) for m in range(3)]
    moment_step(grads, refs[8:11], *refs[11:])


def moment_kernel(grad_ref, *refs):
    moment_step([grad_ref[m] for m in range(3)], refs[:3], *refs[3:])


def residual_kernel(moment_ref, coeffs_ref, in_row_ref, in_col_t_ref, cosines_ref, cosines_t_ref, *outs):
    *residuals, decoded_ref, cells_ref = outs
    side = cosines_ref.shape[0]
    count = residuals[0].shape[0]
    blocks = range(3 * count)
    cosines = cosines_ref[...]
    band = [coeffs_ref[b] * dot(in_row_ref[b], in_col_t_ref[b]) for b in blocks]
    inner = dot3(jnp.concatenate(band, axis=0), cosines)
    inner = jnp.concatenate([inner[b * side : (b + 1) * side] for b in blocks], axis=1)
    decoded = dot3(cosines_t_ref[...], inner)
    for b in blocks:
        kept = decoded[:, b * side : (b + 1) * side]
        decoded_ref[b] = kept
        residuals[b // count][b % count] = moment_ref[b] - kept
    parts = jnp.concatenate(split2(cosines), axis=1)
    for b in blocks:
        cells_ref[b] = dot(in_col_t_ref[b], parts).astype(BF16)


def update_kernel(decoded_ref, other_ref, in_row_ref, cells_ref, cosines_t_ref, *outs):
    side = cosines_t_ref.shape[0]
    count = outs[0].shape[0]
    inner = []
    for b in range(3 * count):
        m, i = b // count, b % count
        hi, lo = split2(sum(other_ref[g, m, i : i + 1, :] for g in range(other_ref.shape[0])))
        in_row = in_row_ref[b]
        upper = in_row * hi
        c_hi, c_lo = cells_ref[b, :, :side], cells_ref[b, :, side:]
        left = jnp.concatenate([upper, in_row * lo, upper], axis=1)
        inner.append(dot(left, jnp.concatenate([c_hi, c_hi, c_lo], axis=0)))
    update = dot3(cosines_t_ref[...], jnp.concatenate(inner, axis=1))
    for b in range(3 * count):
        outs[b // count][b % count] = decoded_ref[b] + update[:, b * side : (b + 1) * side]


def call(kernel, out_shape, flops, *args, scratch=(), in_place={}):
    moved = sum(a.size * a.dtype.itemsize for a in args)
    specs = [
        pl.BlockSpec(memory_space=in_place.get(k, pltpu.VMEM)) for k in range(len(args))
    ]
    return pl.pallas_call(
        kernel,
        out_shape=out_shape,
        in_specs=specs,
        scratch_shapes=list(scratch),
        compiler_params=pltpu.CompilerParams(vmem_limit_bytes=24 * 1024 * 1024),
        cost_estimate=pl.CostEstimate(flops=flops, bytes_accessed=2 * moved, transcendentals=0),
    )(*args)


def ring_perms(count):
    chips = count // 2
    order = list(range(0, chips, 2)) + list(range(1, chips, 2))[::-1]
    forward = [
        (2 * order[p] + c, 2 * order[(p + 1) % chips] + c) for p in range(chips) for c in range(2)
    ]
    return forward, [(b, a) for a, b in forward], chips


def after(kernel, out_shape, flops, band_index, *ahead):
    in_place = dict.fromkeys(range(1, 1 + len(ahead)), pl.ANY)
    return call(kernel, out_shape, flops, band_index, *ahead, in_place=in_place)


def band_tables(band_index, side, *ahead):
    blocks, keep = band_index.shape[0] * band_index.shape[1], band_index.shape[2]
    hots = jax.ShapeDtypeStruct((blocks, side, keep), BF16)
    return after(tables_kernel, (hots, hots), TABLES_FLOPS, band_index, *ahead)


def band_columns(band_index, side, *ahead):
    blocks, keep = band_index.shape[0] * band_index.shape[1], band_index.shape[2]
    hots = jax.ShapeDtypeStruct((blocks, keep, side), BF16)
    return after(columns_kernel, hots, COLUMNS_FLOPS, band_index, *ahead)


def column_moments(x, d, weights, momenta, band_index, cosines, cosines_t, shapes):
    side = weights[0].shape[1]
    rows, width = x.shape
    count = lax.axis_size("fsdp")
    swap = [(f, f ^ 1) for f in range(count)]
    forward, back, chips = ring_perms(count)

    def send(value, perm):
        return lax.ppermute(value, "fsdp", perm)

    xf, db, df, xb = send(x, forward), send(d, back), send(d, forward), send(x, back)
    xs, ds = [x, xf, xb], [d, df, db]
    partner_weights = [send(w, swap) for w in weights]
    pause = call(pause_kernel, jax.ShapeDtypeStruct((8, 128), F32), PAUSE_FLOPS)
    db, pause = lax.optimization_barrier((db, pause))
    arrived = []

    def with_weight(value):
        if len(arrived) == len(partner_weights):
            return value
        value, weight = lax.optimization_barrier((value, partner_weights[len(arrived)]))
        arrived.append(weight)
        return value

    for _ in range(chips // 2 - 2):
        db = with_weight(db)
        xf, db, df, xb = send(xf, forward), send(db, back), send(df, forward), send(xb, back)
        xs += [xf, xb]
        ds += [df, db]
    x_last, d_last = send(xf, forward), send(with_weight(db), back)
    partner_weights[: len(arrived)] = arrived

    def scratch(shards):
        return (
            pltpu.VMEM((shards * rows, width), BF16),
            pltpu.VMEM((shards * rows, width), BF16),
            pltpu.VMEM((6 * side, shards * rows), BF16),
        )

    part = jax.ShapeDtypeStruct((3, side, width), F32)
    early = len(xs) - 2
    own, partner, wgu, wd = call(
        functools.partial(early_kernel, early),
        (
            part,
            part,
            jax.ShapeDtypeStruct((4 * side, width), BF16),
            jax.ShapeDtypeStruct((2 * side, width), BF16),
        ),
        24 * early * rows * width * side,
        *xs[:early],
        *ds[:early],
        *weights,
        *partner_weights,
        pause,
        scratch=scratch(early),
    )
    own, partner = call(
        functools.partial(middle_kernel, 2),
        (part, part),
        24 * 2 * rows * width * side,
        *xs[early:],
        *ds[early:],
        wgu,
        wd,
        own,
        partner,
        scratch=scratch(2),
    )
    got = send(partner, swap)
    x_swap, d_swap = send(x_last, swap), send(d_last, swap)
    in_col_t = band_columns(band_index, side, partner)
    in_row, in_col = band_tables(band_index, side, x_last, d_last)
    moments = call(
        late_kernel,
        shapes,
        10**9,
        x_last,
        x_swap,
        d_last,
        d_swap,
        wgu,
        wd,
        own,
        got,
        *momenta,
        in_row,
        in_col,
        cosines,
        cosines_t,
    )
    return moments, in_row, in_col_t


def shared_column_moments(x, d, weights, momenta, band_index, cosines, cosines_t, shapes):
    gate_weight, up_weight, down_weight = weights
    own = shared_column_grads(x, d, gate_weight, up_weight, down_weight)
    in_col_t = band_columns(band_index, cosines.shape[0], own)
    in_row, in_col = band_tables(band_index, cosines.shape[0], own)
    moments = call(
        moment_kernel,
        shapes,
        0,
        own,
        *momenta,
        in_row,
        in_col,
        cosines,
        cosines_t,
    )
    return moments, in_row, in_col_t


def shared_column_grads(x, d, gate_weight, up_weight, down_weight):
    side = gate_weight.shape[1]
    width = x.shape[1]
    blk_dev = gate_weight.shape[0]
    count = lax.axis_size("fsdp")
    share = width // side // blk_dev
    groups = [list(range(g * share, (g + 1) * share)) for g in range(count // share)]

    def whole(w):
        return lax.all_gather(w, "fsdp", axis=0, tiled=True, axis_index_groups=groups)

    gate, up = whole(gate_weight).reshape(width, side), whole(up_weight).reshape(width, side)
    down = whole(down_weight).transpose(1, 0, 2).reshape(side, width)
    x_all = lax.all_gather(x, "fsdp", axis=0, tiled=True)
    d_all = lax.all_gather(d, "fsdp", axis=0, tiled=True)
    gate_pre = jnp.dot(x_all, gate, preferred_element_type=F32)
    up_pre = jnp.dot(x_all, up, preferred_element_type=F32)
    d_hidden = jnp.dot(d_all, down.T, preferred_element_type=F32)
    sig = jax.nn.sigmoid(gate_pre)
    hidden = (gate_pre * sig * up_pre).astype(BF16)
    d_gate = (d_hidden * up_pre * sig * (1.0 + gate_pre * (1.0 - sig))).astype(BF16)
    d_up = (d_hidden * gate_pre * sig).astype(BF16)
    start = lax.rem(lax.axis_index("fsdp"), share) * blk_dev * side
    x_own = lax.dynamic_slice_in_dim(x_all, start, blk_dev * side, axis=1)
    d_own = lax.dynamic_slice_in_dim(d_all, start, blk_dev * side, axis=1)
    own = jnp.stack(
        [
            jnp.dot(d_gate.T, x_own, preferred_element_type=F32),
            jnp.dot(d_up.T, x_own, preferred_element_type=F32),
            jnp.dot(hidden.T, d_own, preferred_element_type=F32),
        ]
    )
    return own


def per_device(
    x_in, d_out, gate_weight, up_weight, down_weight, mom_gate, mom_up, mom_down, band_index
):
    side = gate_weight.shape[1]
    blk_dev = gate_weight.shape[0]
    row_blocks = x_in.shape[2] // side
    if blk_dev == row_blocks and lax.axis_size("fsdp") % 4 == 0:
        step = column_moments
    else:
        step = shared_column_moments
    cosines, cosines_t = jnp.asarray(dct_table(side)), jnp.asarray(dct_table(side).T)
    blocks = 3 * blk_dev
    dense = jax.ShapeDtypeStruct((blocks, side, side), F32)
    (moment, coeffs, band), in_row, in_col_t = step(
        x_in[0],
        d_out[0],
        (gate_weight, up_weight, down_weight),
        (mom_gate[0], mom_up[0], mom_down[0]),
        band_index,
        cosines,
        cosines_t,
        (dense, dense, jax.ShapeDtypeStruct(band_index.shape, F32)),
    )
    reps = lax.axis_size("rep")
    other = jnp.stack(
        [
            lax.ppermute(band, "rep", [(r, (r + s) % reps) for r in range(reps)])
            for s in range(1, reps)
        ]
    )
    result = jax.ShapeDtypeStruct((blk_dev, side, side), F32)
    flops = 4 * 3 * blocks * side**3
    *residuals, decoded, cells = call(
        residual_kernel,
        (result,) * 3 + (dense, jax.ShapeDtypeStruct((*in_col_t.shape[:2], 2 * side), BF16)),
        flops,
        moment,
        coeffs,
        in_row,
        in_col_t,
        cosines,
        cosines_t,
    )
    updates = call(
        update_kernel, (result,) * 3, flops, decoded, other, in_row, cells, cosines_t
    )
    return (*(r[None] for r in residuals), *updates)


def solution(mesh):
    in_specs = (
        P("rep", "fsdp", None),
        P("rep", "fsdp", None),
        P("fsdp", None, None),
        P("fsdp", None, None),
        P("fsdp", None, None),
        P("rep", "fsdp", None, None),
        P("rep", "fsdp", None, None),
        P("rep", "fsdp", None, None),
        P(None, "fsdp", None),
    )
    out_specs = (
        P("rep", "fsdp", None, None),
        P("rep", "fsdp", None, None),
        P("rep", "fsdp", None, None),
        P("fsdp", None, None),
        P("fsdp", None, None),
        P("fsdp", None, None),
    )
    return jax.shard_map(
        per_device, mesh=mesh, in_specs=in_specs, out_specs=out_specs, check_vma=False
    )
```
